32 devices in a mesh: wide: 8 (over z, y), narrow: 4 (over x, core).
Axes of the slice: x: 2, y: 2, z: 4, core: 2. Of those that a mesh axis runs over, the one named last changes fastest.
Arguments:
- features: bfloat16 [8, 4, 128, 128], P('wide', 'narrow'), may hold values from -6 to 6
- offsets: bfloat16 [8, 4, 2, 128], P('wide', 'narrow'), may hold values from 0 to 1
- counts: int32 [8, 4], P('wide', 'narrow'), may hold values from 64 to 128
- owned_pairs: int32 [8, 4, 8], P('wide', 'narrow'), may hold values from 0 to 1, as said below
- kernels: bfloat16 [8, 128, 128], replicated, may hold values from -0.1875 to 0.1875
- cotangent: bfloat16 [8, 4, 128, 128], P('wide', 'narrow'), may hold values from -6 to 6
Outputs:
- corrected: bfloat16 [8, 4, 128, 128], P('wide', 'narrow')
- grad_features: float32 [8, 4, 128, 128], P('wide', 'narrow')
- grad_kernels: float32 [8, 128, 128], replicated
The draws below stay inside these ranges and needn't reach their ends.
Inputs may be any that keep to these rules, and one draw needn't show every extreme that they name: owned_pairs[x, y, s] = 1 means that the device of cell (x, y) evaluates the pair of tower cell (x, y + a) and plate cell (x + b, y), indices modulo 8 and 4, with (a, b) the s-th of (0,1), (0,-1), (-1,0), (1,0), (-1,1), (1,-1), (1,1), (-1,-1). Each unordered pair of distinct cells whose indices differ by at most one in each dimension is evaluated at most once, by one of its two candidate devices. Some device evaluates all 8.
All inputs are finite; a program needn't handle non-finite values.
Results may differ from the reference program's by a relative error of at most 0.0075.
Values may be sent and summed in bfloat16 or wider, within the bound.
A program may use at most 64 MiB of HBM per device.

```python
import math
from functools import partial
import jax
import jax.numpy as jnp
from jax import lax

C = 128
K = 8
P_SIZE = 128
NW = 8
NN = 4


def draw_owned_pairs(key, part):
    first_key, second_key, third_key, fourth_key, fifth_key = jax.random.split(key, 5)
    band_width = max(NW // 4, 1)
    band_shift = jax.random.randint(first_key, (), 0, NW)
    stripe = (jnp.arange(NW) + band_shift) // band_width % 2
    threshold = 1 + 6 * stripe
    dice_roll = jax.random.randint(second_key, (NW, NN, 4), 0, 8)
    orientation = (dice_roll >= threshold[:, None, None]).astype(jnp.int32)
    listed = jax.random.randint(third_key, (NW, NN, 4), 0, 4) > 0
    flag_table = jnp.where(listed, orientation, 2).astype(jnp.int32)
    hot_col = jax.random.randint(fourth_key, (), 0, NW)
    hot_row = jax.random.randint(fifth_key, (), 0, NN)
    left_col = (hot_col - 1) % NW
    lower_row = (hot_row - 1) % NN
    upper_row = (hot_row + 1) % NN
    flag_table = flag_table.at[hot_col, hot_row, 0].set(0)
    flag_table = flag_table.at[left_col, hot_row, 0].set(1)
    flag_table = flag_table.at[hot_col, lower_row, 1].set(0)
    flag_table = flag_table.at[hot_col, hot_row, 1].set(1)
    flag_table = flag_table.at[hot_col, lower_row, 2].set(0)
    flag_table = flag_table.at[left_col, hot_row, 2].set(1)
    flag_table = flag_table.at[hot_col, upper_row, 3].set(0)
    flag_table = flag_table.at[left_col, hot_row, 3].set(1)
    first_dir = flag_table[:, :, 0]
    second_dir = flag_table[:, :, 1]
    third_dir = flag_table[:, :, 2]
    fourth_dir = flag_table[:, :, 3]
    slot_list = [first_dir == 0, jnp.roll(first_dir, 1, axis=0) == 1, jnp.roll(second_dir, 1, axis=1) == 0, second_dir == 1, jnp.roll(third_dir, 1, axis=1) == 0, jnp.roll(third_dir, 1, axis=0) == 1, jnp.roll(fourth_dir, -1, axis=1) == 0, jnp.roll(fourth_dir, 1, axis=0) == 1]
    return jnp.stack(slot_list, axis=-1).astype(jnp.int32)


def set_ends(values, stream_key, least, high):
    index_at = [jax.random.randint(jax.random.fold_in(stream_key, axis), (), 0, length) for axis, length in enumerate(values.shape)]
    longest = values.shape.index(max(values.shape))
    beside = index_at[:longest] + [(index_at[longest] + 1) % values.shape[longest]] + index_at[longest + 1:]
    return values.at[tuple(index_at)].set(least).at[tuple(beside)].set(high)


def block_scale(own_key, dims, cuts, least, top_value):
    loudness = 1.0
    for dim, shards_of in cuts:
        draws = jax.random.uniform(jax.random.fold_in(jax.random.fold_in(own_key, 6), dim), (shards_of,), jnp.float32, least / len(cuts), top_value / len(cuts))
        loudness = loudness * jnp.repeat(jnp.exp(draws), dims[dim] // shards_of).reshape((-1,) + (1,) * (len(dims) - 1 - dim))
    return loudness


def scatter_about(key, extent, width, reach, cuts=(), held_as=jnp.bfloat16):
    gain = block_scale(key, extent, cuts, -0.22, 0.18) if cuts else 1.0
    entries = jax.random.normal(key, extent, jnp.float32) * width * gain
    return jnp.minimum(jnp.maximum(entries, -reach), reach).astype(held_as)


def setup_inputs(seed: int = 0) -> dict:
    splits = jax.random.split(jax.random.key(seed), 7)
    return {
        "features": scatter_about(splits[0], (NW, NN, P_SIZE, C), 1.0, 6.0, ((0, 8), (1, 4))),
        "offsets": jnp.clip(1.0 * jax.random.uniform(splits[1], (NW, NN, 2, P_SIZE), jnp.float32) ** block_scale(splits[1], (NW, NN, 2, P_SIZE), ((0, 8), (1, 4)), -0.2, 0.2), 0.0, 1.0).astype(jnp.bfloat16),
        "counts": set_ends(jax.random.randint(splits[2], (NW, NN), P_SIZE // 2, P_SIZE + 1), jax.random.fold_in(splits[2], 1), P_SIZE // 2, P_SIZE).astype(jnp.int32),
        "owned_pairs": draw_owned_pairs(jax.random.fold_in(splits[6], 71), 0),
        "kernels": scatter_about(splits[4], (K, C, C), (K * C) ** -0.5, 0.1875),
        "cotangent": scatter_about(splits[5], (NW, NN, P_SIZE, C), 1.0, 6.0, ((0, 8), (1, 4))),
    }


KERNEL_SCALE = 0.0625
SLOT_SHIFTS = ((0, 1), (0, -1), (-1, 0), (1, 0), (-1, 1), (1, -1), (1, 1), (-1, -1))

def round_half(values):
    return lax.optimization_barrier(values.astype(jnp.bfloat16)).astype(jnp.float32)

def kernel_terms(tower_geom, plate_geom, row_shift, col_shift):
    delta_x = plate_geom[..., 0, None, :] + col_shift - tower_geom[..., 0, :, None]
    delta_y = plate_geom[..., 1, None, :] - row_shift - tower_geom[..., 1, :, None]
    square = delta_x * delta_x + delta_y * delta_y
    radius = jnp.sqrt(square)
    window = jnp.square(jnp.maximum(1.0 - square, 0.0))
    weight = KERNEL_SCALE * window * tower_geom[..., 2, :, None] * plate_geom[..., 2, None, :]
    pieces = []
    for level_index in range(4):
        bump_term = weight * jnp.maximum(1.0 - jnp.abs(3.0 * radius - level_index), 0.0)
        pieces.append(bump_term * delta_x)
        pieces.append(bump_term * delta_y)
    return jnp.stack(pieces, axis=-3)

def column_terms(row_shift, col_shift, matrices, inputs):
    tower_geom, plate_geom, tower_h, plate_h, tower_g, plate_g, tower_proj, plate_proj, active = inputs
    kernel_f32 = kernel_terms(tower_geom, plate_geom, row_shift, col_shift) * active[:, None, None, None]
    row_sums = lax.optimization_barrier(jnp.sum(kernel_f32, axis=3))
    col_sums = lax.optimization_barrier(jnp.sum(kernel_f32, axis=2))
    kernel_half = round_half(kernel_f32)
    tower_mix = round_half(row_sums[..., None] * tower_h[:, None] + jnp.einsum('ykij,yjc->ykic', kernel_half, plate_h))
    plate_mix = round_half(jnp.einsum('ykij,yic->ykjc', kernel_half, tower_h) + col_sums[..., None] * plate_h[:, None])
    tower_force = jnp.einsum('ykic,kcd->yid', tower_mix, matrices)
    plate_force = -jnp.einsum('ykjc,kcd->yjd', plate_mix, matrices)
    tower_grad = lax.optimization_barrier(jnp.sum(row_sums[..., None] * tower_proj, axis=1)) - jnp.einsum('ykij,ykjc->yic', kernel_half, plate_proj)
    plate_grad = jnp.einsum('ykij,ykic->yjc', kernel_half, tower_proj) - lax.optimization_barrier(jnp.sum(col_sums[..., None] * plate_proj, axis=1))
    kernel_part = jnp.einsum('ykic,yid->kcd', tower_mix, tower_g) - jnp.einsum('ykjc,yjd->kcd', plate_mix, plate_g)
    return (tower_force, plate_force, tower_grad, plate_grad, kernel_part)

def reference(features, offsets, counts, owned_pairs, kernels, cotangent):
    live_mask = (jnp.arange(P_SIZE, dtype=jnp.int32)[None, None, :] < counts[:, :, None]).astype(jnp.float32)
    geometry = jnp.concatenate([offsets.astype(jnp.float32), live_mask[:, :, None, :]], axis=2)
    hidden = features.astype(jnp.float32)
    upstream = cotangent.astype(jnp.float32)
    matrices = kernels.astype(jnp.float32)
    projected = round_half(jnp.einsum('xyid,kcd->xykic', upstream, matrices))
    force_sum = jnp.zeros(hidden.shape, jnp.float32)
    grad_sum = jnp.zeros(hidden.shape, jnp.float32)
    kernel_sum = jnp.zeros(matrices.shape, jnp.float32)
    shifts = list(SLOT_SHIFTS) + [(0, 0)]
    for slot_index, (row_shift, col_shift) in enumerate(shifts):
        if slot_index < 8:
            active = owned_pairs[:, :, slot_index].astype(jnp.float32)
        else:
            active = jnp.ones(live_mask.shape[:2], jnp.float32)
        inputs = (jnp.roll(geometry, -row_shift, axis=1), jnp.roll(geometry, -col_shift, axis=0), jnp.roll(hidden, -row_shift, axis=1), jnp.roll(hidden, -col_shift, axis=0), jnp.roll(upstream, -row_shift, axis=1), jnp.roll(upstream, -col_shift, axis=0), jnp.roll(projected, -row_shift, axis=1), jnp.roll(projected, -col_shift, axis=0), active)
        tower_force, plate_force, tower_grad, plate_grad, kernel_parts = lax.map(partial(column_terms, row_shift, col_shift, matrices), inputs)
        kernel_sum = kernel_sum + lax.optimization_barrier(jnp.sum(kernel_parts, axis=0))
        force_sum = force_sum + jnp.roll(tower_force, row_shift, axis=1) + jnp.roll(plate_force, col_shift, axis=0)
        grad_sum = grad_sum + jnp.roll(tower_grad, row_shift, axis=1) + jnp.roll(plate_grad, col_shift, axis=0)
    return (force_sum.astype(jnp.bfloat16), grad_sum, kernel_sum / math.sqrt(NW * NN * P_SIZE))
```

```python
import math

import jax
import jax.numpy as jnp
from jax import lax
from jax.experimental import pallas as pl
from jax.experimental.pallas import tpu as pltpu
from jax.sharding import PartitionSpec as P

KERNEL_SCALE = 0.0625
SLOT_SHIFTS = ((0, 1), (0, -1), (-1, 0), (1, 0), (-1, 1), (1, -1), (1, 1), (-1, -1))
AROUND = ((0, 0), (-1, 0), (1, 0), (0, -1), (0, 1), (-1, -1), (-1, 1), (1, -1), (1, 1))
NEAR = 5
FLAGS = 8
CHUNK = 32
F32 = jnp.float32
BF16 = jnp.bfloat16


def spot(dx, dy):
    return AROUND.index((dx, dy))


def make_kernel(nw, nn, particles, channels, levels):
    rows = levels * channels
    rows_n = rows // nn
    rows_w = rows_n // nw
    scattered = rows_w % 16 == 0 and rows_w > 0
    norm = 1.0 / math.sqrt(nw * nn * particles)
    near = NEAR * particles

    def kernel(
        counts_ref, owned_ref, feat_ref, off_ref, kern_ref, cot_ref,
        corrected_ref, grad_ref, weights_ref,
        x_all, geo, s_all, w_acc, rho, own_x, own_y, own_live, z_cat, y_cat,
        w_part, n_in, w_sum, w_in, w_out, n_out,
        x_send, x_recv, g_send, g_recv, ns_send, ns_recv, ws_send, ws_recv,
        wa_send, wa_recv, na_send, na_recv,
    ):
        mw = lax.axis_index("wide")
        mn = lax.axis_index("narrow")

        def wide_peer(step):
            return (lax.rem(mw + step + nw, nw), mn)

        def narrow_peer(step):
            return (mw, lax.rem(mn + step + nn, nn))

        barrier = pltpu.get_barrier_semaphore()
        for d in range(1, nw):
            pl.semaphore_signal(
                barrier, inc=1, device_id=wide_peer(d), device_id_type=pl.DeviceIdType.MESH
            )
        for d in range(1, nn):
            pl.semaphore_signal(
                barrier, inc=1, device_id=narrow_peer(d), device_id_type=pl.DeviceIdType.MESH
            )

        def remote(src, dst, send, recv, peer):
            return pltpu.make_async_remote_copy(
                src_ref=src, dst_ref=dst, send_sem=send, recv_sem=recv,
                device_id=peer, device_id_type=pl.DeviceIdType.MESH,
            )

        x_all[0:particles, 0:channels] = feat_ref[0, 0]
        x_all[0:particles, channels : 2 * channels] = cot_ref[0, 0]
        off = off_ref[0, 0].astype(F32)
        lane = lax.broadcasted_iota(jnp.int32, (1, particles), 1)
        live = (lane < counts_ref[0, 0]).astype(F32)
        geo[0, 0:2, :] = off
        geo[0, 2:3, :] = live
        for s in range(len(SLOT_SHIFTS)):
            geo[0, FLAGS + s : FLAGS + s + 1, :] = jnp.full(
                (1, particles), owned_ref[0, 0, s].astype(F32)
            )

        pl.semaphore_wait(barrier, nw - 1 + nn - 1)

        def block(q):
            return x_all.at[pl.ds(q * particles, particles)]

        geo_copies = {}
        x_copies = {}

        def send_geo(src, slot, peer):
            copy = remote(geo.at[src], geo.at[slot], g_send.at[slot], g_recv.at[slot], peer)
            copy.start()
            geo_copies[slot] = copy

        def send_x(src, slot, peer):
            copy = remote(block(src), block(slot), x_send.at[slot], x_recv.at[slot], peer)
            copy.start()
            x_copies[slot] = copy

        own_sends = [(spot(-d, 0), wide_peer(d)) for d in (1, -1)]
        own_sends += [(spot(0, -d), narrow_peer(d)) for d in (1, -1)]
        for slot, peer in own_sends:
            send_geo(0, slot, peer)
        for slot, peer in own_sends:
            send_x(0, slot, peer)

        own_x[...] = jnp.broadcast_to(off[0:1], (particles, particles)).T
        own_y[...] = jnp.broadcast_to(off[1:2], (particles, particles)).T
        own_live[...] = jnp.broadcast_to(live, (particles, particles)).T

        def pair_kernel(q):
            dx, dy = AROUND[q]
            there = geo[q]
            qx = there[0:1] + float(dx)
            qy = there[1:2] + float(dy)
            weight = there[2:3] * KERNEL_SCALE
            if q == 0:
                weight = weight * 2.0
            else:
                first = FLAGS + SLOT_SHIFTS.index((-dy, dx))
                second = FLAGS + SLOT_SHIFTS.index((dy, -dx))
                weight = weight * (
                    geo[spot(0, dy), first : first + 1] + geo[spot(dx, 0), second : second + 1]
                )

            @pl.loop(0, particles // CHUNK)
            def _(c):
                r = pl.multiple_of(c * CHUNK, CHUNK)
                u = qx - own_x[pl.ds(r, CHUNK), :]
                v = qy - own_y[pl.ds(r, CHUNK), :]
                square = u * u + v * v
                triple = 3.0 * jnp.sqrt(square)
                window = jnp.maximum(1.0 - square, 0.0)
                window = window * window * weight
                wu = window * u
                wv = window * v
                for level in range(levels // 2):
                    bump = jnp.maximum(1.0 - jnp.abs(triple - float(level)), 0.0)
                    for part, value in ((0, wu), (1, wv)):
                        base = (2 * level + part) * particles
                        s_all[pl.ds(base + r, CHUNK), q * particles : (q + 1) * particles] = (
                            bump * value
                        ).astype(BF16)

        pair_kernel(0)
        for dx in (1, -1):
            src = spot(dx, 0)
            geo_copies[src].wait_recv()
            for d in (1, -1):
                send_geo(src, spot(dx, -d), narrow_peer(d))
        for dx in (1, -1):
            src = spot(dx, 0)
            pair_kernel(src)
            x_copies[src].wait_recv()
            for d in (1, -1):
                send_x(src, spot(dx, -d), narrow_peer(d))
        for dy in (1, -1):
            src = spot(0, dy)
            geo_copies[src].wait_recv()
            pair_kernel(src)
        for q in range(NEAR, len(AROUND)):
            geo_copies[q].wait_recv()
            pair_kernel(q)
        rho[...] = jnp.dot(
            s_all[...], jnp.ones((s_all.shape[1], channels), BF16), preferred_element_type=F32
        )
        for dy in (1, -1):
            x_copies[spot(0, dy)].wait_recv()
        w_acc[...] = jnp.dot(s_all[:, 0:near], x_all[0:near, :], preferred_element_type=F32)
        for q in range(NEAR, len(AROUND)):
            x_copies[q].wait_recv()
        w_acc[...] += jnp.dot(s_all[:, near:], x_all[near:, :], preferred_element_type=F32)

        feat = feat_ref[0, 0].astype(F32)
        cot = cot_ref[0, 0]
        cot_f32 = cot.astype(F32)
        for k in range(levels):
            mine = slice(k * particles, (k + 1) * particles)
            lanes = slice(k * channels, (k + 1) * channels)
            r = rho[mine, :]
            z = (r * feat + w_acc[mine, 0:channels]) * own_live[:, 0:1]
            y = (r * cot_f32 - w_acc[mine, channels:]) * own_live[:, 0:1]
            z_cat[:, lanes] = z.astype(BF16)
            y_cat[:, lanes] = y.astype(BF16)
        w_part[...] = (
            lax.dot_general(
                z_cat[...], cot, (((0,), (0,)), ((), ())), preferred_element_type=F32
            )
            .astype(BF16)
            .reshape(nn, rows_n, channels)
        )

        scatter_n = []
        for d in range(1, nn):
            peer = narrow_peer(d)
            copy = remote(
                w_part.at[peer[1]], n_in.at[d - 1], ns_send.at[d - 1], ns_recv.at[d - 1], peer
            )
            copy.start()
            scatter_n.append(copy)

        matrices = kern_ref[...].reshape(rows, channels)
        force = jnp.dot(z_cat[...], matrices, preferred_element_type=F32)
        corrected_ref[0, 0] = force.astype(BF16)
        grad = jnp.zeros((particles, channels), F32)
        for k in range(levels):
            grad += lax.dot_general(
                y_cat[:, k * channels : (k + 1) * channels],
                kern_ref[k],
                (((1,), (1,)), ((), ())),
                preferred_element_type=F32,
            )
        grad_ref[0, 0] = grad

        total = w_part[mn].astype(F32)
        for d in range(1, nn):
            scatter_n[d - 1].wait_recv()
            total += n_in[d - 1].astype(F32)

        scatter_w = []
        gather_w = []
        if scattered:
            w_sum[...] = total.astype(BF16).reshape(nw, rows_w, channels)
            for d in range(1, nw):
                peer = wide_peer(d)
                copy = remote(
                    w_sum.at[peer[0]], w_in.at[d - 1], ws_send.at[d - 1], ws_recv.at[d - 1], peer
                )
                copy.start()
                scatter_w.append(copy)
            piece = w_sum[mw].astype(F32)
            for d in range(1, nw):
                scatter_w[d - 1].wait_recv()
                piece += w_in[d - 1].astype(F32)
            w_out[mw] = (piece * norm).astype(BF16)
            for d in range(1, nw):
                copy = remote(
                    w_out.at[mw], w_out.at[mw], wa_send.at[d - 1], wa_recv.at[d - 1], wide_peer(d)
                )
                copy.start()
                gather_w.append(copy)
            for copy in gather_w:
                copy.wait_recv()
            n_out[mn] = w_out[...].reshape(rows_n, channels)
        else:
            w_in[mw] = total.astype(BF16)
            for d in range(1, nw):
                copy = remote(
                    w_in.at[mw], w_in.at[mw], ws_send.at[d - 1], ws_recv.at[d - 1], wide_peer(d)
                )
                copy.start()
                scatter_w.append(copy)
            for copy in scatter_w:
                copy.wait_recv()
            n_out[mn] = (jnp.sum(w_in[...].astype(F32), axis=0) * norm).astype(BF16)
        gather_n = []
        for d in range(1, nn):
            copy = remote(
                n_out.at[mn], n_out.at[mn], na_send.at[d - 1], na_recv.at[d - 1], narrow_peer(d)
            )
            copy.start()
            gather_n.append(copy)
        for copy in gather_n:
            copy.wait_recv()
        weights_ref[...] = n_out[...].astype(F32).reshape(weights_ref.shape)

        for copies in (geo_copies, x_copies):
            for copy in copies.values():
                copy.wait_send()
        for copies in (scatter_n, scatter_w, gather_w, gather_n):
            for copy in copies:
                copy.wait_send()

    spots = len(AROUND)
    if scattered:
        wide_in = (max(nw - 1, 1), rows_w, channels)
        wide_out = (nw, rows_w, channels)
    else:
        wide_in = (nw, rows_n, channels)
        wide_out = (1, 16, channels)
    dma = pltpu.SemaphoreType.DMA
    scratch = [
        pltpu.VMEM((spots * particles, 2 * channels), BF16),
        pltpu.VMEM((spots, FLAGS + len(SLOT_SHIFTS), particles), F32),
        pltpu.VMEM((levels * particles, spots * particles), BF16),
        pltpu.VMEM((levels * particles, 2 * channels), F32),
        pltpu.VMEM((levels * particles, channels), F32),
        pltpu.VMEM((particles, particles), F32),
        pltpu.VMEM((particles, particles), F32),
        pltpu.VMEM((particles, particles), F32),
        pltpu.VMEM((particles, rows), BF16),
        pltpu.VMEM((particles, rows), BF16),
        pltpu.VMEM((nn, rows_n, channels), BF16),
        pltpu.VMEM((nn - 1, rows_n, channels), BF16),
        pltpu.VMEM(wide_out, BF16),
        pltpu.VMEM(wide_in, BF16),
        pltpu.VMEM(wide_out, BF16),
        pltpu.VMEM((nn, rows_n, channels), BF16),
        dma((spots,)), dma((spots,)), dma((spots,)), dma((spots,)),
        dma((nn - 1,)), dma((nn - 1,)), dma((nw - 1,)), dma((nw - 1,)),
        dma((nw - 1,)), dma((nw - 1,)), dma((nn - 1,)), dma((nn - 1,)),
    ]
    return kernel, scratch


def body(features, offsets, counts, owned_pairs, kernels, cotangent):
    particles, channels = features.shape[2:]
    levels = kernels.shape[0]
    nw, nn = lax.axis_size("wide"), lax.axis_size("narrow")
    kernel, scratch = make_kernel(nw, nn, particles, channels, levels)
    vmem = pl.BlockSpec(memory_space=pltpu.VMEM)
    smem = pl.BlockSpec(memory_space=pltpu.SMEM)
    return pl.pallas_call(
        kernel,
        out_shape=(
            jax.ShapeDtypeStruct(features.shape, BF16),
            jax.ShapeDtypeStruct(features.shape, F32),
            jax.ShapeDtypeStruct(kernels.shape, F32),
        ),
        in_specs=[smem, smem, vmem, vmem, vmem, vmem],
        out_specs=(vmem, vmem, vmem),
        scratch_shapes=scratch,
        compiler_params=pltpu.CompilerParams(
            collective_id=0, has_side_effects=True, vmem_limit_bytes=40 * 1024 * 1024
        ),
        name="antisymmetric_convolution",
    )(counts, owned_pairs, features, offsets, kernels, cotangent)


def solution(mesh):
    placed = (
        P("wide", "narrow", None, None),
        P("wide", "narrow", None, None),
        P("wide", "narrow"),
        P("wide", "narrow", None),
        P(),
        P("wide", "narrow", None, None),
    )
    return jax.shard_map(
        body,
        mesh=mesh,
        in_specs=placed,
        out_specs=(P("wide", "narrow", None, None), P("wide", "narrow", None, None), P()),
        check_vma=False,
    )
```

```python
import math

import jax
import jax.numpy as jnp
from jax import lax
from jax.experimental import pallas as pl
from jax.experimental.pallas import tpu as pltpu
from jax.sharding import PartitionSpec as P

KERNEL_SCALE = 0.0625
SLOT_SHIFTS = ((0, 1), (0, -1), (-1, 0), (1, 0), (-1, 1), (1, -1), (1, 1), (-1, -1))
AROUND = ((0, 0), (-1, 0), (1, 0), (0, -1), (0, 1), (-1, -1), (-1, 1), (1, -1), (1, 1))
NEAR = 5
FLAGS = 8
CHUNK = 32
F32 = jnp.float32
BF16 = jnp.bfloat16


def spot(dx, dy):
    return AROUND.index((dx, dy))


def make_kernel(nw, nn, particles, channels, levels):
    rows = levels * channels
    rows_n = rows // nn
    rows_w = rows_n // nw
    scattered = rows_w % 16 == 0 and rows_w > 0
    norm = 1.0 / math.sqrt(nw * nn * particles)
    near = NEAR * particles
    far_first = sorted(range(1, nn), key=lambda d: -min(d, nn - d))

    def kernel(
        counts_ref, owned_ref, feat_ref, off_ref, kern_ref, cot_ref,
        corrected_ref, grad_ref, n_out,
        f_all, g_all, k_all, geo, s_all, f_acc, g_acc, rho, own_x, own_y, own_live, z_all, y_all,
        w_part, n_in, w_sum, w_in,
        in_sem, f_send, f_recv, g_send, g_recv, p_send, p_recv,
        ns_send, ns_recv, ws_send, ws_recv, wa_send, wa_recv, na_send, na_recv,
    ):
        mw = lax.axis_index("wide")
        mn = lax.axis_index("narrow")

        def wide_peer(step):
            return (lax.rem(mw + step + nw, nw), mn)

        def narrow_peer(step):
            return (mw, lax.rem(mn + step + nn, nn))

        barrier = pltpu.get_barrier_semaphore()
        for d in range(1, nw):
            pl.semaphore_signal(
                barrier, inc=1, device_id=wide_peer(d), device_id_type=pl.DeviceIdType.MESH
            )
        for d in range(1, nn):
            pl.semaphore_signal(
                barrier, inc=1, device_id=narrow_peer(d), device_id_type=pl.DeviceIdType.MESH
            )

        def remote(src, dst, send, recv, peer):
            return pltpu.make_async_remote_copy(
                src_ref=src, dst_ref=dst, send_sem=send, recv_sem=recv,
                device_id=peer, device_id_type=pl.DeviceIdType.MESH,
            )

        def block(ref, q):
            return ref.at[pl.ds(q * particles, particles)]

        feat_in = pltpu.make_async_copy(feat_ref.at[0, 0], block(f_all, 0), in_sem.at[0])
        cot_in = pltpu.make_async_copy(cot_ref.at[0, 0], block(g_all, 0), in_sem.at[1])
        kern_in = pltpu.make_async_copy(kern_ref, k_all, in_sem.at[2])
        feat_in.start()
        cot_in.start()
        kern_in.start()

        off = off_ref[0, 0].astype(F32)
        lane = lax.broadcasted_iota(jnp.int32, (1, particles), 1)
        live = (lane < counts_ref[0, 0]).astype(F32)
        geo[0, 0:2, :] = off
        geo[0, 2:3, :] = live
        for s in range(len(SLOT_SHIFTS)):
            geo[0, FLAGS + s : FLAGS + s + 1, :] = jnp.full(
                (1, particles), owned_ref[0, 0, s].astype(F32)
            )

        pl.semaphore_wait(barrier, nw - 1 + nn - 1)

        geo_copies, f_copies, g_copies = {}, {}, {}

        def send_geo(src, slot, peer):
            copy = remote(geo.at[src], geo.at[slot], p_send.at[slot], p_recv.at[slot], peer)
            copy.start()
            geo_copies[slot] = copy

        def send_f(src, slot, peer):
            copy = remote(
                block(f_all, src), block(f_all, slot), f_send.at[slot], f_recv.at[slot], peer
            )
            copy.start()
            f_copies[slot] = copy

        def send_g(src, slot, peer):
            copy = remote(
                block(g_all, src), block(g_all, slot), g_send.at[slot], g_recv.at[slot], peer
            )
            copy.start()
            g_copies[slot] = copy

        def forward(send, copies):
            for dx in (1, -1):
                copies[spot(dx, 0)].wait_recv()
                for d in (1, -1):
                    send(spot(dx, 0), spot(dx, -d), narrow_peer(d))

        own_sends = [(spot(-d, 0), wide_peer(d)) for d in (1, -1)]
        own_sends += [(spot(0, -d), narrow_peer(d)) for d in (1, -1)]
        for slot, peer in own_sends:
            send_geo(0, slot, peer)
        feat_in.wait()
        for slot, peer in own_sends:
            send_f(0, slot, peer)
        cot_in.wait()
        for slot, peer in own_sends:
            send_g(0, slot, peer)

        own_x[...] = jnp.broadcast_to(off[0:1], (particles, particles)).T
        own_y[...] = jnp.broadcast_to(off[1:2], (particles, particles)).T
        own_live[...] = jnp.broadcast_to(live, (particles, particles)).T

        def pair_kernel(q):
            dx, dy = AROUND[q]
            there = geo[q]
            qx = there[0:1] + float(dx)
            qy = there[1:2] + float(dy)
            weight = there[2:3] * KERNEL_SCALE
            if q == 0:
                weight = weight * 2.0
            else:
                first = FLAGS + SLOT_SHIFTS.index((-dy, dx))
                second = FLAGS + SLOT_SHIFTS.index((dy, -dx))
                weight = weight * (
                    geo[spot(0, dy), first : first + 1] + geo[spot(dx, 0), second : second + 1]
                )

            @pl.loop(0, particles // CHUNK)
            def _(c):
                r = pl.multiple_of(c * CHUNK, CHUNK)
                u = qx - own_x[pl.ds(r, CHUNK), :]
                v = qy - own_y[pl.ds(r, CHUNK), :]
                square = u * u + v * v
                triple = 3.0 * jnp.sqrt(square)
                window = jnp.maximum(1.0 - square, 0.0)
                window = window * window * weight
                wu = window * u
                wv = window * v
                for level in range(levels // 2):
                    bump = jnp.maximum(1.0 - jnp.abs(triple - float(level)), 0.0)
                    for part, value in ((0, wu), (1, wv)):
                        base = (2 * level + part) * particles
                        s_all[pl.ds(base + r, CHUNK), q * particles : (q + 1) * particles] = (
                            bump * value
                        ).astype(BF16)

        pair_kernel(0)
        forward(send_geo, geo_copies)
        pair_kernel(spot(1, 0))
        pair_kernel(spot(-1, 0))
        forward(send_f, f_copies)
        for dy in (1, -1):
            geo_copies[spot(0, dy)].wait_recv()
            pair_kernel(spot(0, dy))
        forward(send_g, g_copies)
        for q in range(NEAR, len(AROUND)):
            geo_copies[q].wait_recv()
            pair_kernel(q)
        rho[...] = jnp.dot(
            s_all[...], jnp.ones((s_all.shape[1], channels), BF16), preferred_element_type=F32
        )
        for dy in (1, -1):
            f_copies[spot(0, dy)].wait_recv()
        f_acc[...] = jnp.dot(s_all[:, 0:near], f_all[0:near, :], preferred_element_type=F32)
        for q in range(NEAR, len(AROUND)):
            f_copies[q].wait_recv()

        feat = f_all[0:particles, :].astype(F32)
        cot = g_all[0:particles, :]
        cot_f32 = cot.astype(F32)

        def finish_z(level, count):
            span = pl.ds(pl.multiple_of(level * particles, particles), count * particles)
            acc = f_acc[span, :] + jnp.dot(
                s_all[span, near:], f_all[near:, :], preferred_element_type=F32
            )
            r = rho[span, :]
            parts = []
            for j in range(count):
                mine = slice(j * particles, (j + 1) * particles)
                z = ((r[mine] * feat + acc[mine]) * own_live[...]).astype(BF16)
                z_all[level + j] = z
                parts.append(
                    lax.dot_general(
                        z, cot, (((0,), (0,)), ((), ())), preferred_element_type=F32
                    ).astype(BF16)
                )
            return jnp.concatenate(parts, axis=0)

        scatter_n = {}

        def send_part(d):
            peer = narrow_peer(d)
            copy = remote(
                w_part.at[peer[1]], n_in.at[d - 1], ns_send.at[d - 1], ns_recv.at[d - 1], peer
            )
            copy.start()
            scatter_n[d] = copy

        each = levels // nn
        if levels % nn == 0:
            for d in far_first + [0]:
                piece = narrow_peer(d)[1]
                w_part[piece] = finish_z(piece * each, each)
                if d:
                    send_part(d)
        else:
            w_part[...] = finish_z(0, levels).reshape(nn, rows_n, channels)
            for d in far_first:
                send_part(d)

        kern_in.wait()
        force = jnp.zeros((particles, channels), F32)
        for k in range(levels):
            force += jnp.dot(z_all[k], k_all[k], preferred_element_type=F32)
        corrected_ref[0, 0] = force.astype(BF16)
        for dy in (1, -1):
            g_copies[spot(0, dy)].wait_recv()
        for q in range(NEAR, len(AROUND)):
            g_copies[q].wait_recv()
        g_acc[...] = jnp.dot(s_all[...], g_all[...], preferred_element_type=F32)
        grad = jnp.zeros((particles, channels), F32)
        for k in range(levels):
            mine = slice(k * particles, (k + 1) * particles)
            y = ((rho[mine, :] * cot_f32 - g_acc[mine, :]) * own_live[...]).astype(BF16)
            grad += lax.dot_general(
                y, k_all[k], (((1,), (1,)), ((), ())), preferred_element_type=F32
            )
        grad_ref[0, 0] = grad

        total = w_part[mn].astype(F32)
        for d in range(1, nn):
            scatter_n[d].wait_recv()
            total += n_in[d - 1].astype(F32)

        scatter_w = []
        gather_w = []
        gather_n = []

        def send_narrow(step):
            at = lax.rem(mw - step + nw, nw) if scattered else 0
            for d in far_first:
                copy = remote(
                    n_out.at[mn, at], n_out.at[mn, at],
                    na_send.at[d - 1, step], na_recv.at[d - 1, step], narrow_peer(d),
                )
                copy.start()
                gather_n.append(copy)

        if scattered:
            w_sum[...] = total.astype(BF16).reshape(nw, rows_w, channels)
            for d in range(1, nw):
                peer = wide_peer(d)
                copy = remote(
                    w_sum.at[peer[0]], w_in.at[d - 1], ws_send.at[d - 1], ws_recv.at[d - 1], peer
                )
                copy.start()
                scatter_w.append(copy)
            piece = w_sum[mw].astype(F32)
            for d in range(1, nw):
                scatter_w[d - 1].wait_recv()
                piece += w_in[d - 1].astype(F32)
            n_out[mn, mw] = (piece * norm).astype(BF16)
            for d in range(1, nw):
                copy = remote(
                    n_out.at[mn, mw], n_out.at[mn, mw],
                    wa_send.at[d - 1], wa_recv.at[d - 1], wide_peer(d),
                )
                copy.start()
                gather_w.append(copy)
            send_narrow(0)
            for step in range(1, nw):
                gather_w[step - 1].wait_recv()
                send_narrow(step)
        else:
            w_in[mw] = total.astype(BF16)
            for d in range(1, nw):
                copy = remote(
                    w_in.at[mw], w_in.at[mw], ws_send.at[d - 1], ws_recv.at[d - 1], wide_peer(d)
                )
                copy.start()
                scatter_w.append(copy)
            for copy in scatter_w:
                copy.wait_recv()
            n_out[mn, 0] = (jnp.sum(w_in[...].astype(F32), axis=0) * norm).astype(BF16)
            send_narrow(0)
        for copy in gather_n:
            copy.wait_recv()

        for copies in (geo_copies, f_copies, g_copies, scatter_n):
            for copy in copies.values():
                copy.wait_send()
        for copies in (scatter_w, gather_w, gather_n):
            for copy in copies:
                copy.wait_send()

    spots = len(AROUND)
    wide_in = (nw - 1, rows_w, channels) if scattered else (nw, rows_n, channels)
    wide_sum = (nw, rows_w, channels) if scattered else (1, 16, channels)
    gathered = (nn, nw, rows_w, channels) if scattered else (nn, 1, rows_n, channels)
    dma = pltpu.SemaphoreType.DMA
    square = pltpu.VMEM((particles, particles), F32)
    scratch = [
        pltpu.VMEM((spots * particles, channels), BF16),
        pltpu.VMEM((spots * particles, channels), BF16),
        pltpu.VMEM((levels, channels, channels), BF16),
        pltpu.VMEM((spots, FLAGS + len(SLOT_SHIFTS), particles), F32),
        pltpu.VMEM((levels * particles, spots * particles), BF16),
        pltpu.VMEM((levels * particles, channels), F32),
        pltpu.VMEM((levels * particles, channels), F32),
        pltpu.VMEM((levels * particles, channels), F32),
        square, square, square,
        pltpu.VMEM((levels, particles, channels), BF16),
        pltpu.VMEM((levels, particles, channels), BF16),
        pltpu.VMEM((nn, rows_n, channels), BF16),
        pltpu.VMEM((nn - 1, rows_n, channels), BF16),
        pltpu.VMEM(wide_sum, BF16),
        pltpu.VMEM(wide_in, BF16),
        dma((3,)),
        dma((spots,)), dma((spots,)), dma((spots,)), dma((spots,)), dma((spots,)), dma((spots,)),
        dma((nn - 1,)), dma((nn - 1,)), dma((nw - 1,)), dma((nw - 1,)),
        dma((nw - 1,)), dma((nw - 1,)),
        dma((nn - 1, gathered[1])), dma((nn - 1, gathered[1])),
    ]
    return kernel, scratch, gathered


def deliver(corrected_in, grad_in, weights_in, corrected_ref, grad_ref, weights_ref, wide, sems):
    copies = [
        pltpu.make_async_copy(grad_in, grad_ref, sems.at[0]),
        pltpu.make_async_copy(corrected_in, corrected_ref, sems.at[1]),
        pltpu.make_async_copy(wide, weights_ref, sems.at[2]),
    ]
    copies[0].start()
    copies[1].start()
    wide[...] = weights_in[...].astype(F32).reshape(wide.shape)
    copies[2].start()
    for copy in copies:
        copy.wait()


def body(features, offsets, counts, owned_pairs, kernels, cotangent):
    particles, channels = features.shape[2:]
    levels = kernels.shape[0]
    nw, nn = lax.axis_size("wide"), lax.axis_size("narrow")
    kernel, scratch, gathered = make_kernel(nw, nn, particles, channels, levels)
    vmem = pl.BlockSpec(memory_space=pltpu.VMEM)
    smem = pl.BlockSpec(memory_space=pltpu.SMEM)
    hbm = pl.BlockSpec(memory_space=pltpu.HBM)
    outs = (
        jax.ShapeDtypeStruct(features.shape, BF16),
        jax.ShapeDtypeStruct(features.shape, F32),
    )
    results = pl.pallas_call(
        kernel,
        out_shape=outs + (jax.ShapeDtypeStruct(gathered, BF16),),
        in_specs=[smem, smem, hbm, vmem, hbm, hbm],
        out_specs=(vmem, vmem, vmem),
        scratch_shapes=scratch,
        compiler_params=pltpu.CompilerParams(
            collective_id=0, has_side_effects=True, vmem_limit_bytes=40 * 1024 * 1024
        ),
        name="antisymmetric_convolution",
    )(counts, owned_pairs, features, offsets, kernels, cotangent)
    return pl.pallas_call(
        deliver,
        out_shape=outs + (jax.ShapeDtypeStruct(kernels.shape, F32),),
        in_specs=[vmem, vmem, vmem],
        out_specs=(hbm, hbm, hbm),
        scratch_shapes=[pltpu.VMEM(kernels.shape, F32), pltpu.SemaphoreType.DMA((3,))],
        compiler_params=pltpu.CompilerParams(vmem_limit_bytes=16 * 1024 * 1024),
        name="deliver",
    )(*results)


def solution(mesh):
    placed = (
        P("wide", "narrow", None, None),
        P("wide", "narrow", None, None),
        P("wide", "narrow"),
        P("wide", "narrow", None),
        P(),
        P("wide", "narrow", None, None),
    )
    return jax.shard_map(
        body,
        mesh=mesh,
        in_specs=placed,
        out_specs=(P("wide", "narrow", None, None), P("wide", "narrow", None, None), P()),
        check_vma=False,
    )
```

```python
import math

import jax
import jax.numpy as jnp
from jax import lax
from jax.experimental import pallas as pl
from jax.experimental.pallas import tpu as pltpu
from jax.sharding import PartitionSpec as P

KERNEL_SCALE = 0.0625
SLOT_SHIFTS = ((0, 1), (0, -1), (-1, 0), (1, 0), (-1, 1), (1, -1), (1, 1), (-1, -1))
AROUND = ((0, 0), (-1, 0), (1, 0), (0, -1), (0, 1), (-1, -1), (-1, 1), (1, -1), (1, 1))
NEAR = 5
FLAGS = 8
CHUNK = 32
VMEM_BYTES = 56 * 1024 * 1024
F32 = jnp.float32
BF16 = jnp.bfloat16


def spot(dx, dy):
    return AROUND.index((dx, dy))


def make_kernel(nw, nn, particles, channels, levels):
    rows = levels * channels
    rows_n = rows // nn
    rows_w = rows_n // nw
    scattered = rows_w % 16 == 0 and rows_w > 0
    norm = 1.0 / math.sqrt(nw * nn * particles)
    near = NEAR * particles
    gathered = (nn, nw, rows_w, channels) if scattered else (nn, 1, rows_n, channels)
    far_first = sorted(range(1, nn), key=lambda d: -min(d, nn - d))

    def kernel(
        counts_ref, owned_ref, feat_ref, off_ref, kern_ref, cot_ref,
        corrected_ref, grad_ref, n_out,
        f_all, g_all, k_all, geo, rows_of, s_all, f_acc, own_x, own_y, own_live, z_all,
        force_out, grad_out, w_part, n_in, w_sum, w_in, w_out,
        in_sem, out_sem, f_send, f_recv, g_send, g_recv, p_send, p_recv,
        ns_send, ns_recv, ws_send, ws_recv, wa_send, wa_recv, na_send, na_recv,
    ):
        mw = lax.axis_index("wide")
        mn = lax.axis_index("narrow")

        def wide_peer(step):
            return (lax.rem(mw + step + nw, nw), mn)

        def narrow_peer(step):
            return (mw, lax.rem(mn + step + nn, nn))

        barrier = pltpu.get_barrier_semaphore()
        for d in range(1, nw):
            pl.semaphore_signal(
                barrier, inc=1, device_id=wide_peer(d), device_id_type=pl.DeviceIdType.MESH
            )
        for d in range(1, nn):
            pl.semaphore_signal(
                barrier, inc=1, device_id=narrow_peer(d), device_id_type=pl.DeviceIdType.MESH
            )

        def remote(src, dst, send, recv, peer):
            return pltpu.make_async_remote_copy(
                src_ref=src, dst_ref=dst, send_sem=send, recv_sem=recv,
                device_id=peer, device_id_type=pl.DeviceIdType.MESH,
            )

        def block(ref, q):
            return ref.at[pl.ds(q * particles, particles)]

        feat_in = pltpu.make_async_copy(feat_ref.at[0, 0], block(f_all, 0), in_sem.at[0])
        cot_in = pltpu.make_async_copy(cot_ref.at[0, 0], block(g_all, 0), in_sem.at[1])
        kern_in = pltpu.make_async_copy(kern_ref, k_all, in_sem.at[2])
        feat_in.start()
        cot_in.start()
        kern_in.start()

        off = off_ref[0, 0].astype(F32)
        lane = lax.broadcasted_iota(jnp.int32, (1, particles), 1)
        live = (lane < counts_ref[0, 0]).astype(F32)
        geo[0, 0:2, :] = off
        geo[0, 2:3, :] = live
        for s in range(len(SLOT_SHIFTS)):
            geo[0, FLAGS + s : FLAGS + s + 1, :] = jnp.full(
                (1, particles), owned_ref[0, 0, s].astype(F32)
            )

        pl.semaphore_wait(barrier, nw - 1 + nn - 1)

        geo_copies, f_copies, g_copies = {}, {}, {}

        def send_geo(src, slot, peer):
            copy = remote(geo.at[src], geo.at[slot], p_send.at[slot], p_recv.at[slot], peer)
            copy.start()
            geo_copies[slot] = copy

        def send_f(src, slot, peer):
            copy = remote(
                block(f_all, src), block(f_all, slot), f_send.at[slot], f_recv.at[slot], peer
            )
            copy.start()
            f_copies[slot] = copy

        def send_g(src, slot, peer):
            copy = remote(
                block(g_all, src), block(g_all, slot), g_send.at[slot], g_recv.at[slot], peer
            )
            copy.start()
            g_copies[slot] = copy

        def forward(send, copies):
            for dx in (1, -1):
                copies[spot(dx, 0)].wait_recv()
                for d in (1, -1):
                    send(spot(dx, 0), spot(dx, -d), narrow_peer(d))

        own_sends = [(spot(-d, 0), wide_peer(d)) for d in (1, -1)]
        own_sends += [(spot(0, -d), narrow_peer(d)) for d in (1, -1)]
        for slot, peer in own_sends:
            send_geo(0, slot, peer)
        feat_in.wait()
        for slot, peer in own_sends:
            send_f(0, slot, peer)
        cot_in.wait()
        for slot, peer in own_sends:
            send_g(0, slot, peer)

        own_x[...] = jnp.broadcast_to(off[0:1], (particles, particles)).T
        own_y[...] = jnp.broadcast_to(off[1:2], (particles, particles)).T
        own_live[...] = jnp.broadcast_to(live, (particles, particles)).T

        def pair_rows(q):
            dx, dy = AROUND[q]
            there = geo[q]
            weight = there[2:3] * KERNEL_SCALE
            if q == 0:
                weight = weight * 2.0
            else:
                first = FLAGS + SLOT_SHIFTS.index((-dy, dx))
                second = FLAGS + SLOT_SHIFTS.index((dy, -dx))
                weight = weight * (
                    geo[spot(0, dy), first : first + 1] + geo[spot(dx, 0), second : second + 1]
                )
            rows_of[q, 0:1, :] = there[0:1] + float(dx)
            rows_of[q, 1:2, :] = there[1:2] + float(dy)
            rows_of[q, 2:3, :] = weight

        def pair_kernels(start, stop):
            for q in range(start, stop):
                pair_rows(q)
            chunks = particles // CHUNK

            @pl.loop(start * chunks, stop * chunks)
            def _(step):
                q = step // chunks
                r = pl.multiple_of(step % chunks * CHUNK, CHUNK)
                lanes = pl.ds(pl.multiple_of(q * particles, particles), particles)
                u = rows_of[q, 0:1, :] - own_x[pl.ds(r, CHUNK), :]
                v = rows_of[q, 1:2, :] - own_y[pl.ds(r, CHUNK), :]
                square = u * u + v * v
                triple = 3.0 * jnp.sqrt(square)
                window = jnp.maximum(1.0 - square, 0.0)
                window = window * window * rows_of[q, 2:3, :]
                wu = window * u
                wv = window * v
                for level in range(levels // 2):
                    bump = jnp.maximum(1.0 - jnp.abs(triple - float(level)), 0.0)
                    for part, value in ((0, wu), (1, wv)):
                        base = (2 * level + part) * particles
                        s_all[pl.ds(base + r, CHUNK), lanes] = (bump * value).astype(BF16)

        pair_kernels(0, 1)
        forward(send_geo, geo_copies)
        for dy in (1, -1):
            geo_copies[spot(0, dy)].wait_recv()
        pair_kernels(1, NEAR)
        forward(send_f, f_copies)
        for q in range(NEAR, len(AROUND)):
            geo_copies[q].wait_recv()
        pair_kernels(NEAR, len(AROUND))
        forward(send_g, g_copies)
        for dy in (1, -1):
            f_copies[spot(0, dy)].wait_recv()

        def with_ones(blocks):
            return jnp.concatenate([blocks, jnp.ones(blocks.shape, BF16)], axis=1)

        @pl.loop(0, levels // 2)
        def _(step):
            span = pl.ds(pl.multiple_of(step * 2 * particles, 2 * particles), 2 * particles)
            f_acc[span, :] = jnp.dot(
                s_all[span, 0:near], with_ones(f_all[0:near, :]), preferred_element_type=F32
            )

        for q in range(NEAR, len(AROUND)):
            f_copies[q].wait_recv()

        def finish_z(level, count):
            span = pl.ds(pl.multiple_of(level * particles, particles), count * particles)
            acc = f_acc[span, :] + jnp.dot(
                s_all[span, near:], with_ones(f_all[near:, :]), preferred_element_type=F32
            )
            f_acc[span, channels:] = acc[:, channels:]
            feat = f_all[0:particles, :].astype(F32)
            parts = []
            for j in range(count):
                mine = acc[j * particles : (j + 1) * particles]
                z = ((mine[:, channels:] * feat + mine[:, 0:channels]) * own_live[...]).astype(BF16)
                z_all[level + j] = z
                parts.append(
                    lax.dot_general(
                        z, g_all[0:particles, :], (((0,), (0,)), ((), ())),
                        preferred_element_type=F32,
                    ).astype(BF16)
                )
            return jnp.concatenate(parts, axis=0)

        def part_copy(d):
            peer = narrow_peer(d)
            return remote(
                w_part.at[peer[1]], n_in.at[d - 1], ns_send.at[d - 1], ns_recv.at[d - 1], peer
            )

        if levels % nn == 0:
            each = levels // nn

            @pl.loop(1, nn + 1)
            def _(d):
                piece = narrow_peer(d)[1]
                w_part[piece] = finish_z(piece * each, each)

                @pl.when(d < nn)
                def _():
                    part_copy(d).start()
        else:
            split = nn // levels
            assert split * levels == nn

            @pl.loop(0, levels)
            def _(level):
                part = finish_z(level, 1)
                for j in range(split):
                    w_part[level * split + j] = part[j * rows_n : (j + 1) * rows_n]

            @pl.loop(1, nn)
            def _(d):
                part_copy(d).start()

        kern_in.wait()
        for dy in (1, -1):
            g_copies[spot(0, dy)].wait_recv()
        for q in range(NEAR, len(AROUND)):
            g_copies[q].wait_recv()
        force_out[...] = jnp.zeros_like(force_out)
        grad_out[...] = jnp.zeros_like(grad_out)

        @pl.loop(0, levels)
        def _(k):
            span = pl.ds(pl.multiple_of(k * particles, particles), particles)
            force_out[...] += jnp.dot(z_all[k], k_all[k], preferred_element_type=F32)
            acc = jnp.dot(s_all[span, :], g_all[...], preferred_element_type=F32)
            own = f_acc[span, channels:] * g_all[0:particles, :].astype(F32)
            y = ((own - acc) * own_live[...]).astype(BF16)
            grad_out[...] += lax.dot_general(
                y, k_all[k], (((1,), (1,)), ((), ())), preferred_element_type=F32
            )

        corrected_out = f_all.at[pl.ds(0, particles)]
        for copies in (f_copies, g_copies, geo_copies):
            for copy in copies.values():
                copy.wait_send()
        corrected_out[...] = force_out[...].astype(BF16)
        force_copy = pltpu.make_async_copy(corrected_out, corrected_ref.at[0, 0], out_sem.at[0])
        grad_copy = pltpu.make_async_copy(grad_out, grad_ref.at[0, 0], out_sem.at[1])
        force_copy.start()
        grad_copy.start()

        total = w_part[mn].astype(F32)
        for d in range(1, nn):
            part_copy(d).wait_recv()
            total += n_in[d - 1].astype(F32)

        def row_copy(d, step):
            at = lax.rem(mw - step + nw, nw) if scattered else 0
            return remote(
                w_out.at[at], n_out.at[mn, at],
                na_send.at[d - 1, step], na_recv.at[d - 1, step], narrow_peer(d),
            )

        def send_row(step):
            for d in far_first:
                row_copy(d, step).start()

        if scattered:

            def scatter_copy(d):
                peer = wide_peer(d)
                return remote(
                    w_sum.at[peer[0]], w_in.at[d - 1], ws_send.at[d - 1], ws_recv.at[d - 1], peer
                )

            def column_copy(d):
                return remote(
                    w_out.at[mw], w_out.at[mw],
                    wa_send.at[d - 1], wa_recv.at[d - 1], wide_peer(d),
                )

            w_sum[...] = total.astype(BF16).reshape(nw, rows_w, channels)
            for d in range(1, nw):
                scatter_copy(d).start()
            piece = w_sum[mw].astype(F32)
            for d in range(1, nw):
                scatter_copy(d).wait_recv()
                piece += w_in[d - 1].astype(F32)
            w_out[mw] = (piece * norm).astype(BF16)
            for d in range(1, nw):
                column_copy(d).start()
            send_row(0)

            @pl.loop(1, nw)
            def _(step):
                column_copy(step).wait_recv()
                send_row(step)

            @pl.loop(1, nw)
            def _(d):
                scatter_copy(d).wait_send()
                column_copy(d).wait_send()
        else:

            def scatter_copy(d):
                return remote(
                    w_in.at[mw], w_in.at[mw], ws_send.at[d - 1], ws_recv.at[d - 1], wide_peer(d)
                )

            w_in[mw] = total.astype(BF16)

            @pl.loop(1, nw)
            def _(d):
                scatter_copy(d).start()

            @pl.loop(1, nw)
            def _(d):
                scatter_copy(d).wait()

            w_out[0] = (jnp.sum(w_in[...].astype(F32), axis=0) * norm).astype(BF16)
            send_row(0)
        own_copy = pltpu.make_async_copy(w_out, n_out.at[mn], out_sem.at[2])
        own_copy.start()

        @pl.loop(1, nn)
        def _(d):
            part_copy(d).wait_send()

        @pl.loop(0, gathered[1])
        def _(step):
            for d in range(1, nn):
                row_copy(d, step).wait()

        force_copy.wait()
        grad_copy.wait()
        own_copy.wait()

    spots = len(AROUND)
    wide_in = (nw - 1, rows_w, channels) if scattered else (nw, rows_n, channels)
    wide_sum = (nw, rows_w, channels) if scattered else (1, 16, channels)
    dma = pltpu.SemaphoreType.DMA
    square = pltpu.VMEM((particles, particles), F32)
    block_sum = pltpu.VMEM((particles, channels), F32)
    scratch = [
        pltpu.VMEM((spots * particles, channels), BF16),
        pltpu.VMEM((spots * particles, channels), BF16),
        pltpu.VMEM((levels, channels, channels), BF16),
        pltpu.VMEM((spots, FLAGS + len(SLOT_SHIFTS), particles), F32),
        pltpu.VMEM((spots, FLAGS, particles), F32),
        pltpu.VMEM((levels * particles, spots * particles), BF16),
        pltpu.VMEM((levels * particles, 2 * channels), F32),
        square, square, square,
        pltpu.VMEM((levels, particles, channels), BF16),
        block_sum, block_sum,
        pltpu.VMEM((nn, rows_n, channels), BF16),
        pltpu.VMEM((nn - 1, rows_n, channels), BF16),
        pltpu.VMEM(wide_sum, BF16),
        pltpu.VMEM(wide_in, BF16),
        pltpu.VMEM(gathered[1:], BF16),
        dma((3,)), dma((3,)),
        dma((spots,)), dma((spots,)), dma((spots,)), dma((spots,)), dma((spots,)), dma((spots,)),
        dma((nn - 1,)), dma((nn - 1,)), dma((nw - 1,)), dma((nw - 1,)),
        dma((nw - 1,)), dma((nw - 1,)),
        dma((nn - 1, gathered[1])), dma((nn - 1, gathered[1])),
    ]
    return kernel, scratch, gathered


def deliver(
    corrected_in, grad_in, weights_in, corrected_ref, grad_ref, weights_ref, narrow, wide, sems
):
    load = pltpu.make_async_copy(weights_in, narrow, sems.at[0])
    copies = [
        pltpu.make_async_copy(grad_in, grad_ref, sems.at[1]),
        pltpu.make_async_copy(corrected_in, corrected_ref, sems.at[2]),
        pltpu.make_async_copy(wide, weights_ref, sems.at[3]),
    ]
    load.start()
    copies[0].start()
    copies[1].start()
    load.wait()
    wide[...] = narrow[...].astype(F32).reshape(wide.shape)
    copies[2].start()
    for copy in copies:
        copy.wait()


def body(features, offsets, counts, owned_pairs, kernels, cotangent):
    particles, channels = features.shape[2:]
    levels = kernels.shape[0]
    nw, nn = lax.axis_size("wide"), lax.axis_size("narrow")
    kernel, scratch, gathered = make_kernel(nw, nn, particles, channels, levels)
    vmem = pl.BlockSpec(memory_space=pltpu.VMEM)
    smem = pl.BlockSpec(memory_space=pltpu.SMEM)
    hbm = pl.BlockSpec(memory_space=pltpu.HBM)
    outs = (
        jax.ShapeDtypeStruct(features.shape, BF16),
        jax.ShapeDtypeStruct(features.shape, F32),
    )
    results = pl.pallas_call(
        kernel,
        out_shape=outs + (jax.ShapeDtypeStruct(gathered, BF16),),
        in_specs=[smem, smem, hbm, vmem, hbm, hbm],
        out_specs=(hbm, hbm, hbm),
        scratch_shapes=scratch,
        compiler_params=pltpu.CompilerParams(
            collective_id=0, has_side_effects=True, vmem_limit_bytes=VMEM_BYTES
        ),
        name="antisymmetric_convolution",
    )(counts, owned_pairs, features, offsets, kernels, cotangent)
    return pl.pallas_call(
        deliver,
        out_shape=outs + (jax.ShapeDtypeStruct(kernels.shape, F32),),
        in_specs=[hbm, hbm, hbm],
        out_specs=(hbm, hbm, hbm),
        scratch_shapes=[
            pltpu.VMEM(gathered, BF16),
            pltpu.VMEM(kernels.shape, F32),
            pltpu.SemaphoreType.DMA((4,)),
        ],
        compiler_params=pltpu.CompilerParams(vmem_limit_bytes=VMEM_BYTES),
        name="deliver",
    )(*results)


def solution(mesh):
    placed = (
        P("wide", "narrow", None, None),
        P("wide", "narrow", None, None),
        P("wide", "narrow"),
        P("wide", "narrow", None),
        P(),
        P("wide", "narrow", None, None),
    )
    return jax.shard_map(
        body,
        mesh=mesh,
        in_specs=placed,
        out_specs=(P("wide", "narrow", None, None), P("wide", "narrow", None, None), P()),
        check_vma=False,
    )
```

```python
import math

import jax
import jax.numpy as jnp
from jax import lax
from jax.experimental import pallas as pl
from jax.experimental.pallas import tpu as pltpu
from jax.sharding import PartitionSpec as P

KERNEL_SCALE = 0.0625
SLOT_SHIFTS = ((0, 1), (0, -1), (-1, 0), (1, 0), (-1, 1), (1, -1), (1, 1), (-1, -1))
AROUND = ((0, 0), (-1, 0), (1, 0), (0, -1), (0, 1), (-1, -1), (-1, 1), (1, -1), (1, 1))
NEAR = 5
FLAGS = 8
CHUNK = 64
TINY = 1e-30
VMEM_BYTES = 56 * 1024 * 1024
F32 = jnp.float32
BF16 = jnp.bfloat16


def spot(dx, dy):
    return AROUND.index((dx, dy))


def make_kernel(nw, nn, particles, channels, levels):
    rows = levels * channels
    rows_n = rows // nn
    rows_w = rows_n // nw
    scattered = rows_w % 16 == 0 and rows_w > 0
    norm = 1.0 / math.sqrt(nw * nn * particles)
    near = NEAR * particles
    gathered = (nn, nw, rows_w, channels) if scattered else (nn, 1, rows_n, channels)
    far_first = sorted(range(1, nn), key=lambda d: -min(d, nn - d))

    def kernel(
        counts_ref, owned_ref, feat_ref, off_ref, kern_ref, cot_ref,
        corrected_ref, grad_ref, n_out,
        f_all, g_all, k_all, geo, rows_of, s_all, f_acc, own_x, own_y, own_live, z_all,
        force_out, grad_out, w_part, n_in, w_sum, w_in, w_out,
        in_sem, out_sem, f_send, f_recv, g_send, g_recv, p_send, p_recv,
        ns_send, ns_recv, ws_send, ws_recv, wa_send, wa_recv, na_send, na_recv,
    ):
        mw = lax.axis_index("wide")
        mn = lax.axis_index("narrow")

        def wide_peer(step):
            return (lax.rem(mw + step + nw, nw), mn)

        def narrow_peer(step):
            return (mw, lax.rem(mn + step + nn, nn))

        barrier = pltpu.get_barrier_semaphore()
        for d in range(1, nw):
            pl.semaphore_signal(
                barrier, inc=1, device_id=wide_peer(d), device_id_type=pl.DeviceIdType.MESH
            )
        for d in range(1, nn):
            pl.semaphore_signal(
                barrier, inc=1, device_id=narrow_peer(d), device_id_type=pl.DeviceIdType.MESH
            )

        def remote(src, dst, send, recv, peer):
            return pltpu.make_async_remote_copy(
                src_ref=src, dst_ref=dst, send_sem=send, recv_sem=recv,
                device_id=peer, device_id_type=pl.DeviceIdType.MESH,
            )

        def block(ref, q):
            return ref.at[pl.ds(q * particles, particles)]

        feat_in = pltpu.make_async_copy(feat_ref.at[0, 0], block(f_all, 0), in_sem.at[0])
        cot_in = pltpu.make_async_copy(cot_ref.at[0, 0], block(g_all, 0), in_sem.at[1])
        kern_in = pltpu.make_async_copy(kern_ref, k_all, in_sem.at[2])
        feat_in.start()
        cot_in.start()
        kern_in.start()

        off = off_ref[0, 0].astype(F32)
        lane = lax.broadcasted_iota(jnp.int32, (1, particles), 1)
        live = (lane < counts_ref[0, 0]).astype(F32)
        geo[0, 0:2, :] = off
        geo[0, 2:3, :] = live
        for s in range(len(SLOT_SHIFTS)):
            geo[0, FLAGS + s : FLAGS + s + 1, :] = jnp.full(
                (1, particles), owned_ref[0, 0, s].astype(F32)
            )

        pl.semaphore_wait(barrier, nw - 1 + nn - 1)

        geo_copies, f_copies, g_copies = {}, {}, {}

        def send_geo(src, slot, peer):
            copy = remote(geo.at[src], geo.at[slot], p_send.at[slot], p_recv.at[slot], peer)
            copy.start()
            geo_copies[slot] = copy

        def send_f(src, slot, peer):
            copy = remote(
                block(f_all, src), block(f_all, slot), f_send.at[slot], f_recv.at[slot], peer
            )
            copy.start()
            f_copies[slot] = copy

        def send_g(src, slot, peer):
            copy = remote(
                block(g_all, src), block(g_all, slot), g_send.at[slot], g_recv.at[slot], peer
            )
            copy.start()
            g_copies[slot] = copy

        def forward(send, copies):
            for dx in (1, -1):
                copies[spot(dx, 0)].wait_recv()
                for d in (1, -1):
                    send(spot(dx, 0), spot(dx, -d), narrow_peer(d))

        own_sends = [(spot(-d, 0), wide_peer(d)) for d in (1, -1)]
        own_sends += [(spot(0, -d), narrow_peer(d)) for d in (1, -1)]
        for slot, peer in own_sends:
            send_geo(0, slot, peer)
        feat_in.wait()
        for slot, peer in own_sends:
            send_f(0, slot, peer)
        cot_in.wait()
        for slot, peer in own_sends:
            send_g(0, slot, peer)

        own_x[...] = jnp.broadcast_to(off[0:1], (particles, particles)).T
        own_y[...] = jnp.broadcast_to(off[1:2], (particles, particles)).T
        own_live[...] = jnp.broadcast_to(live, (particles, particles)).T

        def pair_rows(q):
            dx, dy = AROUND[q]
            there = geo[q]
            weight = there[2:3] * KERNEL_SCALE
            if q == 0:
                weight = weight * 2.0
            else:
                first = FLAGS + SLOT_SHIFTS.index((-dy, dx))
                second = FLAGS + SLOT_SHIFTS.index((dy, -dx))
                weight = weight * (
                    geo[spot(0, dy), first : first + 1] + geo[spot(dx, 0), second : second + 1]
                )
            rows_of[q, 0:1, :] = there[0:1] + float(dx)
            rows_of[q, 1:2, :] = there[1:2] + float(dy)
            rows_of[q, 2:3, :] = weight

        def pair_kernels(start, stop):
            for q in range(start, stop):
                pair_rows(q)
            chunks = particles // CHUNK

            @pl.loop(start * chunks, stop * chunks)
            def _(step):
                q = step // chunks
                r = pl.multiple_of(step % chunks * CHUNK, CHUNK)
                lanes = pl.ds(pl.multiple_of(q * particles, particles), particles)
                u = rows_of[q, 0:1, :] - own_x[pl.ds(r, CHUNK), :]
                v = rows_of[q, 1:2, :] - own_y[pl.ds(r, CHUNK), :]
                square = u * u + v * v
                triple = 3.0 * (square * lax.rsqrt(jnp.maximum(square, TINY)))
                window = jnp.maximum(1.0 - square, 0.0)
                window = window * window * rows_of[q, 2:3, :]
                wu = window * u
                wv = window * v
                for level in range(levels // 2):
                    bump = jnp.maximum(1.0 - jnp.abs(triple - float(level)), 0.0)
                    for part, value in ((0, wu), (1, wv)):
                        base = (2 * level + part) * particles
                        s_all[pl.ds(base + r, CHUNK), lanes] = (bump * value).astype(BF16)

        pair_kernels(0, 1)
        forward(send_geo, geo_copies)
        for dy in (1, -1):
            geo_copies[spot(0, dy)].wait_recv()
        pair_kernels(1, NEAR)
        forward(send_f, f_copies)
        for q in range(NEAR, len(AROUND)):
            geo_copies[q].wait_recv()
        pair_kernels(NEAR, len(AROUND))
        forward(send_g, g_copies)
        for dy in (1, -1):
            f_copies[spot(0, dy)].wait_recv()

        def with_ones(blocks):
            return jnp.concatenate([blocks, jnp.ones(blocks.shape, BF16)], axis=1)

        @pl.loop(0, levels // 2)
        def _(step):
            span = pl.ds(pl.multiple_of(step * 2 * particles, 2 * particles), 2 * particles)
            f_acc[span, :] = jnp.dot(
                s_all[span, 0:near], with_ones(f_all[0:near, :]), preferred_element_type=F32
            )

        for q in range(NEAR, len(AROUND)):
            f_copies[q].wait_recv()

        def finish_z(level, count):
            span = pl.ds(pl.multiple_of(level * particles, particles), count * particles)
            acc = f_acc[span, :] + jnp.dot(
                s_all[span, near:], with_ones(f_all[near:, :]), preferred_element_type=F32
            )
            f_acc[span, channels:] = acc[:, channels:]
            feat = f_all[0:particles, :].astype(F32)
            parts = []
            for j in range(count):
                mine = acc[j * particles : (j + 1) * particles]
                z = ((mine[:, channels:] * feat + mine[:, 0:channels]) * own_live[...]).astype(BF16)
                z_all[level + j] = z
                parts.append(
                    lax.dot_general(
                        z, g_all[0:particles, :], (((0,), (0,)), ((), ())),
                        preferred_element_type=F32,
                    ).astype(BF16)
                )
            return jnp.concatenate(parts, axis=0)

        def part_copy(d):
            peer = narrow_peer(d)
            return remote(
                w_part.at[peer[1]], n_in.at[d - 1], ns_send.at[d - 1], ns_recv.at[d - 1], peer
            )

        if levels % nn == 0:
            each = levels // nn

            @pl.loop(1, nn + 1)
            def _(d):
                piece = narrow_peer(d)[1]
                w_part[piece] = finish_z(piece * each, each)

                @pl.when(d < nn)
                def _():
                    part_copy(d).start()
        else:
            split = nn // levels
            assert split * levels == nn

            @pl.loop(0, levels)
            def _(level):
                part = finish_z(level, 1)
                for j in range(split):
                    w_part[level * split + j] = part[j * rows_n : (j + 1) * rows_n]

            @pl.loop(1, nn)
            def _(d):
                part_copy(d).start()

        kern_in.wait()
        for dy in (1, -1):
            g_copies[spot(0, dy)].wait_recv()
        for q in range(NEAR, len(AROUND)):
            g_copies[q].wait_recv()
        force_out[...] = jnp.zeros_like(force_out)
        grad_out[...] = jnp.zeros_like(grad_out)

        def outputs_of(k):
            span = pl.ds(pl.multiple_of(k * particles, particles), particles)
            force_out[...] += jnp.dot(z_all[k], k_all[k], preferred_element_type=F32)
            acc = jnp.dot(s_all[span, :], g_all[...], preferred_element_type=F32)
            own = f_acc[span, channels:] * g_all[0:particles, :].astype(F32)
            y = ((own - acc) * own_live[...]).astype(BF16)
            grad_out[...] += lax.dot_general(
                y, k_all[k], (((1,), (1,)), ((), ())), preferred_element_type=F32
            )

        cuts = [0, levels * 3 // 8, levels * 6 // 8, levels]

        def outputs_stage(stage):
            pl.loop(cuts[stage], cuts[stage + 1])(outputs_of)

        def send_outputs():
            corrected_out = f_all.at[pl.ds(0, particles)]
            for copies in (f_copies, g_copies, geo_copies):
                for copy in copies.values():
                    copy.wait_send()
            corrected_out[...] = force_out[...].astype(BF16)
            force_copy = pltpu.make_async_copy(corrected_out, corrected_ref.at[0, 0], out_sem.at[0])
            grad_copy = pltpu.make_async_copy(grad_out, grad_ref.at[0, 0], out_sem.at[1])
            force_copy.start()
            grad_copy.start()
            return force_copy, grad_copy

        outputs_stage(0)

        total = w_part[mn].astype(F32)
        for d in range(1, nn):
            part_copy(d).wait_recv()
            total += n_in[d - 1].astype(F32)

        def row_copy(d, step):
            at = lax.rem(mw - step + nw, nw) if scattered else 0
            return remote(
                w_out.at[at], n_out.at[mn, at],
                na_send.at[d - 1, step], na_recv.at[d - 1, step], narrow_peer(d),
            )

        def send_row(step):
            for d in far_first:
                row_copy(d, step).start()

        if scattered:

            def scatter_copy(d):
                peer = wide_peer(d)
                return remote(
                    w_sum.at[peer[0]], w_in.at[d - 1], ws_send.at[d - 1], ws_recv.at[d - 1], peer
                )

            def column_copy(d):
                return remote(
                    w_out.at[mw], w_out.at[mw],
                    wa_send.at[d - 1], wa_recv.at[d - 1], wide_peer(d),
                )

            w_sum[...] = total.astype(BF16).reshape(nw, rows_w, channels)
            for d in range(1, nw):
                scatter_copy(d).start()
            outputs_stage(1)
            piece = w_sum[mw].astype(F32)
            for d in range(1, nw):
                scatter_copy(d).wait_recv()
                piece += w_in[d - 1].astype(F32)
            w_out[mw] = (piece * norm).astype(BF16)
            for d in range(1, nw):
                column_copy(d).start()
            send_row(0)
            outputs_stage(2)
            force_copy, grad_copy = send_outputs()

            @pl.loop(1, nw)
            def _(step):
                column_copy(step).wait_recv()
                send_row(step)

            @pl.loop(1, nw)
            def _(d):
                scatter_copy(d).wait_send()
                column_copy(d).wait_send()
        else:

            def scatter_copy(d):
                return remote(
                    w_in.at[mw], w_in.at[mw], ws_send.at[d - 1], ws_recv.at[d - 1], wide_peer(d)
                )

            w_in[mw] = total.astype(BF16)

            @pl.loop(1, nw)
            def _(d):
                scatter_copy(d).start()

            @pl.loop(1, nw)
            def _(d):
                scatter_copy(d).wait()

            outputs_stage(1)
            outputs_stage(2)
            force_copy, grad_copy = send_outputs()
            w_out[0] = (jnp.sum(w_in[...].astype(F32), axis=0) * norm).astype(BF16)
            send_row(0)
        own_copy = pltpu.make_async_copy(w_out, n_out.at[mn], out_sem.at[2])
        own_copy.start()

        @pl.loop(1, nn)
        def _(d):
            part_copy(d).wait_send()

        @pl.loop(0, gathered[1])
        def _(step):
            for d in range(1, nn):
                row_copy(d, step).wait()

        force_copy.wait()
        grad_copy.wait()
        own_copy.wait()

    spots = len(AROUND)
    wide_in = (nw - 1, rows_w, channels) if scattered else (nw, rows_n, channels)
    wide_sum = (nw, rows_w, channels) if scattered else (1, 16, channels)
    dma = pltpu.SemaphoreType.DMA
    square = pltpu.VMEM((particles, particles), F32)
    block_sum = pltpu.VMEM((particles, channels), F32)
    scratch = [
        pltpu.VMEM((spots * particles, channels), BF16),
        pltpu.VMEM((spots * particles, channels), BF16),
        pltpu.VMEM((levels, channels, channels), BF16),
        pltpu.VMEM((spots, FLAGS + len(SLOT_SHIFTS), particles), F32),
        pltpu.VMEM((spots, FLAGS, particles), F32),
        pltpu.VMEM((levels * particles, spots * particles), BF16),
        pltpu.VMEM((levels * particles, 2 * channels), F32),
        square, square, square,
        pltpu.VMEM((levels, particles, channels), BF16),
        block_sum, block_sum,
        pltpu.VMEM((nn, rows_n, channels), BF16),
        pltpu.VMEM((nn - 1, rows_n, channels), BF16),
        pltpu.VMEM(wide_sum, BF16),
        pltpu.VMEM(wide_in, BF16),
        pltpu.VMEM(gathered[1:], BF16),
        dma((3,)), dma((3,)),
        dma((spots,)), dma((spots,)), dma((spots,)), dma((spots,)), dma((spots,)), dma((spots,)),
        dma((nn - 1,)), dma((nn - 1,)), dma((nw - 1,)), dma((nw - 1,)),
        dma((nw - 1,)), dma((nw - 1,)),
        dma((nn - 1, gathered[1])), dma((nn - 1, gathered[1])),
    ]
    return kernel, scratch, gathered


def deliver(
    corrected_in, grad_in, weights_in, corrected_ref, grad_ref, weights_ref,
    corrected, grad, narrow, wide, sems,
):
    loads = [
        pltpu.make_async_copy(weights_in, narrow, sems.at[0]),
        pltpu.make_async_copy(grad_in, grad, sems.at[1]),
        pltpu.make_async_copy(corrected_in, corrected, sems.at[2]),
    ]
    copies = [
        pltpu.make_async_copy(wide, weights_ref, sems.at[3]),
        pltpu.make_async_copy(grad, grad_ref, sems.at[4]),
        pltpu.make_async_copy(corrected, corrected_ref, sems.at[5]),
    ]
    for copy in loads:
        copy.start()
    loads[0].wait()
    wide[...] = narrow[...].astype(F32).reshape(wide.shape)
    copies[0].start()
    for load, copy in zip(loads[1:], copies[1:]):
        load.wait()
        copy.start()
    for copy in copies:
        copy.wait()


def body(features, offsets, counts, owned_pairs, kernels, cotangent):
    particles, channels = features.shape[2:]
    levels = kernels.shape[0]
    nw, nn = lax.axis_size("wide"), lax.axis_size("narrow")
    kernel, scratch, gathered = make_kernel(nw, nn, particles, channels, levels)
    vmem = pl.BlockSpec(memory_space=pltpu.VMEM)
    smem = pl.BlockSpec(memory_space=pltpu.SMEM)
    hbm = pl.BlockSpec(memory_space=pltpu.HBM)
    outs = (
        jax.ShapeDtypeStruct(features.shape, BF16),
        jax.ShapeDtypeStruct(features.shape, F32),
    )
    results = pl.pallas_call(
        kernel,
        out_shape=outs + (jax.ShapeDtypeStruct(gathered, BF16),),
        in_specs=[smem, smem, hbm, vmem, hbm, hbm],
        out_specs=(hbm, hbm, hbm),
        scratch_shapes=scratch,
        compiler_params=pltpu.CompilerParams(
            collective_id=0, has_side_effects=True, vmem_limit_bytes=VMEM_BYTES
        ),
        name="antisymmetric_convolution",
    )(counts, owned_pairs, features, offsets, kernels, cotangent)
    return pl.pallas_call(
        deliver,
        out_shape=outs + (jax.ShapeDtypeStruct(kernels.shape, F32),),
        in_specs=[hbm, hbm, hbm],
        out_specs=(hbm, hbm, hbm),
        scratch_shapes=[
            pltpu.VMEM(features.shape, BF16),
            pltpu.VMEM(features.shape, F32),
            pltpu.VMEM(gathered, BF16),
            pltpu.VMEM(kernels.shape, F32),
            pltpu.SemaphoreType.DMA((6,)),
        ],
        compiler_params=pltpu.CompilerParams(vmem_limit_bytes=VMEM_BYTES),
        name="deliver",
    )(*results)


def solution(mesh):
    placed = (
        P("wide", "narrow", None, None),
        P("wide", "narrow", None, None),
        P("wide", "narrow"),
        P("wide", "narrow", None),
        P(),
        P("wide", "narrow", None, None),
    )
    return jax.shard_map(
        body,
        mesh=mesh,
        in_specs=placed,
        out_specs=(P("wide", "narrow", None, None), P("wide", "narrow", None, None), P()),
        check_vma=False,
    )
```

```python
import math

import jax
import jax.numpy as jnp
from jax import lax
from jax.experimental import pallas as pl
from jax.experimental.pallas import tpu as pltpu
from jax.sharding import PartitionSpec as P

KERNEL_SCALE = 0.0625
SLOT_SHIFTS = ((0, 1), (0, -1), (-1, 0), (1, 0), (-1, 1), (1, -1), (1, 1), (-1, -1))
AROUND = ((0, 0), (-1, 0), (1, 0), (0, -1), (0, 1), (-1, -1), (-1, 1), (1, -1), (1, 1))
NEAR = 5
FLAGS = 8
CHUNK = 64
TINY = 1e-30
VMEM_BYTES = 56 * 1024 * 1024
F32 = jnp.float32
BF16 = jnp.bfloat16


def spot(dx, dy):
    return AROUND.index((dx, dy))


def make_kernel(nw, nn, particles, channels, levels):
    rows = levels * channels
    rows_n = rows // nn
    rows_w = rows_n // nw
    scattered = rows_w % 16 == 0 and rows_w > 0
    norm = 1.0 / math.sqrt(nw * nn * particles)
    near = NEAR * particles
    gathered = (nn, nw, rows_w, channels) if scattered else (nn, 1, rows_n, channels)
    far_first = sorted(range(1, nn), key=lambda d: -min(d, nn - d))

    def kernel(
        counts_ref, owned_ref, feat_ref, off_ref, kern_ref, cot_ref,
        corrected_ref, grad_ref, n_out,
        f_all, g_all, k_all, geo, rows_of, s_all, f_acc, own_x, own_y, own_live, z_all,
        force_out, grad_out, w_part, n_in, w_sum, w_in, w_out,
        in_sem, out_sem, f_send, f_recv, g_send, g_recv, p_send, p_recv,
        ns_send, ns_recv, ws_send, ws_recv, wa_send, wa_recv, na_send, na_recv,
    ):
        mw = lax.axis_index("wide")
        mn = lax.axis_index("narrow")

        def wide_peer(step):
            return (lax.rem(mw + step + nw, nw), mn)

        def narrow_peer(step):
            return (mw, lax.rem(mn + step + nn, nn))

        barrier = pltpu.get_barrier_semaphore()
        for d in range(1, nw):
            pl.semaphore_signal(
                barrier, inc=1, device_id=wide_peer(d), device_id_type=pl.DeviceIdType.MESH
            )
        for d in range(1, nn):
            pl.semaphore_signal(
                barrier, inc=1, device_id=narrow_peer(d), device_id_type=pl.DeviceIdType.MESH
            )

        def remote(src, dst, send, recv, peer):
            return pltpu.make_async_remote_copy(
                src_ref=src, dst_ref=dst, send_sem=send, recv_sem=recv,
                device_id=peer, device_id_type=pl.DeviceIdType.MESH,
            )

        def block(ref, q):
            return ref.at[pl.ds(q * particles, particles)]

        feat_in = pltpu.make_async_copy(feat_ref.at[0, 0], block(f_all, 0), in_sem.at[0])
        cot_in = pltpu.make_async_copy(cot_ref.at[0, 0], block(g_all, 0), in_sem.at[1])
        kern_in = pltpu.make_async_copy(kern_ref, k_all, in_sem.at[2])
        feat_in.start()
        cot_in.start()
        kern_in.start()

        off = off_ref[0, 0].astype(F32)
        lane = lax.broadcasted_iota(jnp.int32, (1, particles), 1)
        live = (lane < counts_ref[0, 0]).astype(F32)
        geo[0, 0:2, :] = off
        geo[0, 2:3, :] = live
        for s in range(len(SLOT_SHIFTS)):
            geo[0, FLAGS + s : FLAGS + s + 1, :] = jnp.full(
                (1, particles), owned_ref[0, 0, s].astype(F32)
            )

        pl.semaphore_wait(barrier, nw - 1 + nn - 1)

        geo_copies, f_copies, g_copies = {}, {}, {}

        def send_geo(src, slot, peer):
            copy = remote(geo.at[src], geo.at[slot], p_send.at[slot], p_recv.at[slot], peer)
            copy.start()
            geo_copies[slot] = copy

        def send_f(src, slot, peer):
            held = block(f_all, src) if src else feat_ref.at[0, 0]
            copy = remote(held, block(f_all, slot), f_send.at[slot], f_recv.at[slot], peer)
            copy.start()
            f_copies[slot] = copy

        def send_g(src, slot, peer):
            held = block(g_all, src) if src else cot_ref.at[0, 0]
            copy = remote(held, block(g_all, slot), g_send.at[slot], g_recv.at[slot], peer)
            copy.start()
            g_copies[slot] = copy

        def forward(send, copies):
            for dx in (1, -1):
                copies[spot(dx, 0)].wait_recv()
                for d in (1, -1):
                    send(spot(dx, 0), spot(dx, -d), narrow_peer(d))

        own_sends = [(spot(-d, 0), wide_peer(d)) for d in (1, -1)]
        own_sends += [(spot(0, -d), narrow_peer(d)) for d in (1, -1)]
        for slot, peer in own_sends:
            send_geo(0, slot, peer)
        for slot, peer in own_sends:
            send_f(0, slot, peer)
        for slot, peer in own_sends:
            send_g(0, slot, peer)
        feat_in.wait()
        cot_in.wait()

        own_x[...] = jnp.broadcast_to(off[0:1], (particles, particles)).T
        own_y[...] = jnp.broadcast_to(off[1:2], (particles, particles)).T
        own_live[...] = jnp.broadcast_to(live, (particles, particles)).T

        def pair_rows(q):
            dx, dy = AROUND[q]
            there = geo[q]
            weight = there[2:3] * KERNEL_SCALE
            if q == 0:
                weight = weight * 2.0
            else:
                first = FLAGS + SLOT_SHIFTS.index((-dy, dx))
                second = FLAGS + SLOT_SHIFTS.index((dy, -dx))
                weight = weight * (
                    geo[spot(0, dy), first : first + 1] + geo[spot(dx, 0), second : second + 1]
                )
            rows_of[q, 0:1, :] = there[0:1] + float(dx)
            rows_of[q, 1:2, :] = there[1:2] + float(dy)
            rows_of[q, 2:3, :] = weight

        def pair_kernels(start, stop):
            for q in range(start, stop):
                pair_rows(q)
            chunks = particles // CHUNK

            @pl.loop(start * chunks, stop * chunks)
            def _(step):
                q = step // chunks
                r = pl.multiple_of(step % chunks * CHUNK, CHUNK)
                lanes = pl.ds(pl.multiple_of(q * particles, particles), particles)
                u = rows_of[q, 0:1, :] - own_x[pl.ds(r, CHUNK), :]
                v = rows_of[q, 1:2, :] - own_y[pl.ds(r, CHUNK), :]
                square = u * u + v * v
                triple = 3.0 * (square * lax.rsqrt(jnp.maximum(square, TINY)))
                window = jnp.maximum(1.0 - square, 0.0)
                window = window * window * rows_of[q, 2:3, :]
                wu = window * u
                wv = window * v
                for level in range(levels // 2):
                    bump = jnp.maximum(1.0 - jnp.abs(triple - float(level)), 0.0)
                    for part, value in ((0, wu), (1, wv)):
                        base = (2 * level + part) * particles
                        s_all[pl.ds(base + r, CHUNK), lanes] = (bump * value).astype(BF16)

        pair_kernels(0, 1)
        forward(send_geo, geo_copies)
        for dy in (1, -1):
            geo_copies[spot(0, dy)].wait_recv()
        pair_kernels(1, NEAR)
        forward(send_f, f_copies)
        for q in range(NEAR, len(AROUND)):
            geo_copies[q].wait_recv()
        pair_kernels(NEAR, len(AROUND))
        forward(send_g, g_copies)
        for dy in (1, -1):
            f_copies[spot(0, dy)].wait_recv()

        def with_ones(blocks):
            return jnp.concatenate([blocks, jnp.ones(blocks.shape, BF16)], axis=1)

        @pl.loop(0, levels // 2)
        def _(step):
            span = pl.ds(pl.multiple_of(step * 2 * particles, 2 * particles), 2 * particles)
            f_acc[span, :] = jnp.dot(
                s_all[span, 0:near], with_ones(f_all[0:near, :]), preferred_element_type=F32
            )

        for q in range(NEAR, len(AROUND)):
            f_copies[q].wait_recv()

        def finish_z(level, count):
            span = pl.ds(pl.multiple_of(level * particles, particles), count * particles)
            acc = f_acc[span, :] + jnp.dot(
                s_all[span, near:], with_ones(f_all[near:, :]), preferred_element_type=F32
            )
            f_acc[span, channels:] = acc[:, channels:]
            feat = f_all[0:particles, :].astype(F32)
            parts = []
            for j in range(count):
                mine = acc[j * particles : (j + 1) * particles]
                z = ((mine[:, channels:] * feat + mine[:, 0:channels]) * own_live[...]).astype(BF16)
                z_all[level + j] = z
                parts.append(
                    lax.dot_general(
                        z, g_all[0:particles, :], (((0,), (0,)), ((), ())),
                        preferred_element_type=F32,
                    ).astype(BF16)
                )
            return jnp.concatenate(parts, axis=0)

        def part_copy(d):
            peer = narrow_peer(d)
            return remote(
                w_part.at[peer[1]], n_in.at[d - 1], ns_send.at[d - 1], ns_recv.at[d - 1], peer
            )

        if levels % nn == 0:
            each = levels // nn

            turn = 1 - 2 * lax.rem(mn, 2)

            @pl.loop(0, nn)
            def _(step):
                d = lax.rem(nn // 2 + nn + turn * step, nn)
                piece = narrow_peer(d)[1]
                w_part[piece] = finish_z(piece * each, each)

                @pl.when(d > 0)
                def _():
                    part_copy(d).start()
        else:
            split = nn // levels
            assert split * levels == nn

            @pl.loop(0, levels)
            def _(level):
                part = finish_z(level, 1)
                for j in range(split):
                    w_part[level * split + j] = part[j * rows_n : (j + 1) * rows_n]

            @pl.loop(1, nn)
            def _(d):
                part_copy(d).start()

        kern_in.wait()
        for dy in (1, -1):
            g_copies[spot(0, dy)].wait_recv()
        for q in range(NEAR, len(AROUND)):
            g_copies[q].wait_recv()
        force_out[...] = jnp.zeros_like(force_out)
        grad_out[...] = jnp.zeros_like(grad_out)

        def outputs_of(k):
            span = pl.ds(pl.multiple_of(k * particles, particles), particles)
            force_out[...] += jnp.dot(z_all[k], k_all[k], preferred_element_type=F32)
            acc = jnp.dot(s_all[span, :], g_all[...], preferred_element_type=F32)
            own = f_acc[span, channels:] * g_all[0:particles, :].astype(F32)
            y = ((own - acc) * own_live[...]).astype(BF16)
            grad_out[...] += lax.dot_general(
                y, k_all[k], (((1,), (1,)), ((), ())), preferred_element_type=F32
            )

        cuts = [0, levels // 4, levels * 5 // 8, levels]

        def outputs_stage(stage):
            pl.loop(cuts[stage], cuts[stage + 1])(outputs_of)

        def send_outputs():
            corrected_out = f_all.at[pl.ds(0, particles)]
            for copies in (f_copies, g_copies, geo_copies):
                for copy in copies.values():
                    copy.wait_send()
            corrected_out[...] = force_out[...].astype(BF16)
            force_copy = pltpu.make_async_copy(corrected_out, corrected_ref.at[0, 0], out_sem.at[0])
            grad_copy = pltpu.make_async_copy(grad_out, grad_ref.at[0, 0], out_sem.at[1])
            force_copy.start()
            grad_copy.start()
            return force_copy, grad_copy

        outputs_stage(0)

        total = w_part[mn].astype(F32)
        for d in range(1, nn):
            part_copy(d).wait_recv()
            total += n_in[d - 1].astype(F32)

        def row_copy(d, step):
            at = lax.rem(mw - step + nw, nw) if scattered else 0
            return remote(
                w_out.at[at], n_out.at[mn, at],
                na_send.at[d - 1, step], na_recv.at[d - 1, step], narrow_peer(d),
            )

        def send_row(step):
            for d in far_first:
                row_copy(d, step).start()

        if scattered:

            def scatter_copy(d):
                peer = wide_peer(d)
                return remote(
                    w_sum.at[peer[0]], w_in.at[d - 1], ws_send.at[d - 1], ws_recv.at[d - 1], peer
                )

            def column_copy(d):
                return remote(
                    w_out.at[mw], w_out.at[mw],
                    wa_send.at[d - 1], wa_recv.at[d - 1], wide_peer(d),
                )

            w_sum[...] = total.astype(BF16).reshape(nw, rows_w, channels)
            for d in range(1, nw):
                scatter_copy(d).start()
            outputs_stage(1)
            piece = w_sum[mw].astype(F32)
            for d in range(1, nw):
                scatter_copy(d).wait_recv()
                piece += w_in[d - 1].astype(F32)
            w_out[mw] = (piece * norm).astype(BF16)
            for d in range(1, nw):
                column_copy(d).start()
            send_row(0)
            outputs_stage(2)
            force_copy, grad_copy = send_outputs()

            @pl.loop(1, nw)
            def _(step):
                column_copy(step).wait_recv()
                send_row(step)

            @pl.loop(1, nw)
            def _(d):
                scatter_copy(d).wait_send()
                column_copy(d).wait_send()
        else:

            def scatter_copy(d):
                return remote(
                    w_in.at[mw], w_in.at[mw], ws_send.at[d - 1], ws_recv.at[d - 1], wide_peer(d)
                )

            w_in[mw] = total.astype(BF16)

            @pl.loop(1, nw)
            def _(d):
                scatter_copy(d).start()

            @pl.loop(1, nw)
            def _(d):
                scatter_copy(d).wait()

            outputs_stage(1)
            outputs_stage(2)
            force_copy, grad_copy = send_outputs()
            w_out[0] = (jnp.sum(w_in[...].astype(F32), axis=0) * norm).astype(BF16)
            send_row(0)
        own_copy = pltpu.make_async_copy(w_out, n_out.at[mn], out_sem.at[2])
        own_copy.start()

        @pl.loop(1, nn)
        def _(d):
            part_copy(d).wait_send()

        @pl.loop(0, gathered[1])
        def _(step):
            for d in range(1, nn):
                row_copy(d, step).wait()

        force_copy.wait()
        grad_copy.wait()
        own_copy.wait()

    spots = len(AROUND)
    wide_in = (nw - 1, rows_w, channels) if scattered else (nw, rows_n, channels)
    wide_sum = (nw, rows_w, channels) if scattered else (1, 16, channels)
    dma = pltpu.SemaphoreType.DMA
    square = pltpu.VMEM((particles, particles), F32)
    block_sum = pltpu.VMEM((particles, channels), F32)
    scratch = [
        pltpu.VMEM((spots * particles, channels), BF16),
        pltpu.VMEM((spots * particles, channels), BF16),
        pltpu.VMEM((levels, channels, channels), BF16),
        pltpu.VMEM((spots, FLAGS + len(SLOT_SHIFTS), particles), F32),
        pltpu.VMEM((spots, FLAGS, particles), F32),
        pltpu.VMEM((levels * particles, spots * particles), BF16),
        pltpu.VMEM((levels * particles, 2 * channels), F32),
        square, square, square,
        pltpu.VMEM((levels, particles, channels), BF16),
        block_sum, block_sum,
        pltpu.VMEM((nn, rows_n, channels), BF16),
        pltpu.VMEM((nn - 1, rows_n, channels), BF16),
        pltpu.VMEM(wide_sum, BF16),
        pltpu.VMEM(wide_in, BF16),
        pltpu.VMEM(gathered[1:], BF16),
        dma((3,)), dma((3,)),
        dma((spots,)), dma((spots,)), dma((spots,)), dma((spots,)), dma((spots,)), dma((spots,)),
        dma((nn - 1,)), dma((nn - 1,)), dma((nw - 1,)), dma((nw - 1,)),
        dma((nw - 1,)), dma((nw - 1,)),
        dma((nn - 1, gathered[1])), dma((nn - 1, gathered[1])),
    ]
    return kernel, scratch, gathered


def deliver(
    corrected_in, grad_in, weights_in, corrected_ref, grad_ref, weights_ref,
    corrected, grad, narrow, wide, sems,
):
    loads = [
        pltpu.make_async_copy(weights_in, narrow, sems.at[0]),
        pltpu.make_async_copy(grad_in, grad, sems.at[1]),
        pltpu.make_async_copy(corrected_in, corrected, sems.at[2]),
    ]
    copies = [
        pltpu.make_async_copy(wide, weights_ref, sems.at[3]),
        pltpu.make_async_copy(grad, grad_ref, sems.at[4]),
        pltpu.make_async_copy(corrected, corrected_ref, sems.at[5]),
    ]
    for copy in loads:
        copy.start()
    loads[0].wait()
    wide[...] = narrow[...].astype(F32).reshape(wide.shape)
    copies[0].start()
    for load, copy in zip(loads[1:], copies[1:]):
        load.wait()
        copy.start()
    for copy in copies:
        copy.wait()


def body(features, offsets, counts, owned_pairs, kernels, cotangent):
    particles, channels = features.shape[2:]
    levels = kernels.shape[0]
    nw, nn = lax.axis_size("wide"), lax.axis_size("narrow")
    kernel, scratch, gathered = make_kernel(nw, nn, particles, channels, levels)
    vmem = pl.BlockSpec(memory_space=pltpu.VMEM)
    smem = pl.BlockSpec(memory_space=pltpu.SMEM)
    hbm = pl.BlockSpec(memory_space=pltpu.HBM)
    outs = (
        jax.ShapeDtypeStruct(features.shape, BF16),
        jax.ShapeDtypeStruct(features.shape, F32),
    )
    results = pl.pallas_call(
        kernel,
        out_shape=outs + (jax.ShapeDtypeStruct(gathered, BF16),),
        in_specs=[smem, smem, hbm, vmem, hbm, hbm],
        out_specs=(hbm, hbm, hbm),
        scratch_shapes=scratch,
        compiler_params=pltpu.CompilerParams(
            collective_id=0, has_side_effects=True, vmem_limit_bytes=VMEM_BYTES
        ),
        name="antisymmetric_convolution",
    )(counts, owned_pairs, features, offsets, kernels, cotangent)
    return pl.pallas_call(
        deliver,
        out_shape=outs + (jax.ShapeDtypeStruct(kernels.shape, F32),),
        in_specs=[hbm, hbm, hbm],
        out_specs=(hbm, hbm, hbm),
        scratch_shapes=[
            pltpu.VMEM(features.shape, BF16),
            pltpu.VMEM(features.shape, F32),
            pltpu.VMEM(gathered, BF16),
            pltpu.VMEM(kernels.shape, F32),
            pltpu.SemaphoreType.DMA((6,)),
        ],
        compiler_params=pltpu.CompilerParams(vmem_limit_bytes=VMEM_BYTES),
        name="deliver",
    )(*results)


def solution(mesh):
    placed = (
        P("wide", "narrow", None, None),
        P("wide", "narrow", None, None),
        P("wide", "narrow"),
        P("wide", "narrow", None),
        P(),
        P("wide", "narrow", None, None),
    )
    return jax.shard_map(
        body,
        mesh=mesh,
        in_specs=placed,
        out_specs=(P("wide", "narrow", None, None), P("wide", "narrow", None, None), P()),
        check_vma=False,
    )
```

```python
import math

import jax
import jax.numpy as jnp
from jax import lax
from jax.experimental import pallas as pl
from jax.experimental.pallas import tpu as pltpu
from jax.sharding import PartitionSpec as P

KERNEL_SCALE = 0.0625
SLOT_SHIFTS = ((0, 1), (0, -1), (-1, 0), (1, 0), (-1, 1), (1, -1), (1, 1), (-1, -1))
AROUND = ((0, 0), (-1, 0), (1, 0), (0, -1), (0, 1), (-1, -1), (-1, 1), (1, -1), (1, 1))
NEAR = 5
FLAGS = 8
CHUNK = 64
TINY = 1e-30
VMEM_BYTES = 56 * 1024 * 1024
F32 = jnp.float32
BF16 = jnp.bfloat16


def spot(dx, dy):
    return AROUND.index((dx, dy))


def make_kernel(nw, nn, particles, channels, levels):
    rows = levels * channels
    rows_n = rows // nn
    rows_w = rows_n // nw
    scattered = rows_w % 16 == 0 and rows_w > 0
    norm = 1.0 / math.sqrt(nw * nn * particles)
    near = NEAR * particles
    gathered = (nn, nw, rows_w, channels) if scattered else (nn, 1, rows_n, channels)
    far_first = sorted(range(1, nn), key=lambda d: -min(d, nn - d))

    def kernel(
        counts_ref, owned_ref, feat_ref, off_ref, kern_ref, cot_ref,
        corrected_ref, grad_ref, n_out,
        f_all, g_all, k_all, geo, rows_of, s_all, f_acc, own_x, own_y, own_live, z_all,
        force_out, grad_out, w_part, n_in, w_sum, w_in, w_out,
        in_sem, out_sem, f_send, f_recv, g_send, g_recv, p_send, p_recv,
        ns_send, ns_recv, ws_send, ws_recv, wa_send, wa_recv, na_send, na_recv,
    ):
        mw = lax.axis_index("wide")
        mn = lax.axis_index("narrow")

        def wide_peer(step):
            return (lax.rem(mw + step + nw, nw), mn)

        def narrow_peer(step):
            return (mw, lax.rem(mn + step + nn, nn))

        barrier = pltpu.get_barrier_semaphore()
        for d in range(1, nw):
            pl.semaphore_signal(
                barrier, inc=1, device_id=wide_peer(d), device_id_type=pl.DeviceIdType.MESH
            )
        for d in range(1, nn):
            pl.semaphore_signal(
                barrier, inc=1, device_id=narrow_peer(d), device_id_type=pl.DeviceIdType.MESH
            )

        def remote(src, dst, send, recv, peer):
            return pltpu.make_async_remote_copy(
                src_ref=src, dst_ref=dst, send_sem=send, recv_sem=recv,
                device_id=peer, device_id_type=pl.DeviceIdType.MESH,
            )

        def block(ref, q):
            return ref.at[pl.ds(q * particles, particles)]

        feat_in = pltpu.make_async_copy(feat_ref.at[0, 0], block(f_all, 0), in_sem.at[0])
        cot_in = pltpu.make_async_copy(cot_ref.at[0, 0], block(g_all, 0), in_sem.at[1])
        kern_in = pltpu.make_async_copy(kern_ref, k_all, in_sem.at[2])
        feat_in.start()
        cot_in.start()
        kern_in.start()

        off = off_ref[0, 0].astype(F32)
        lane = lax.broadcasted_iota(jnp.int32, (1, particles), 1)
        live = (lane < counts_ref[0, 0]).astype(F32)
        geo[0, 0:2, :] = off
        geo[0, 2:3, :] = live
        for s in range(len(SLOT_SHIFTS)):
            geo[0, FLAGS + s : FLAGS + s + 1, :] = jnp.full(
                (1, particles), owned_ref[0, 0, s].astype(F32)
            )

        pl.semaphore_wait(barrier, nw - 1 + nn - 1)

        geo_copies, f_copies, g_copies = {}, {}, {}

        def send_geo(src, slot, peer):
            copy = remote(geo.at[src], geo.at[slot], p_send.at[slot], p_recv.at[slot], peer)
            copy.start()
            geo_copies[slot] = copy

        def send_f(src, slot, peer):
            copy = remote(
                block(f_all, src), block(f_all, slot), f_send.at[slot], f_recv.at[slot], peer
            )
            copy.start()
            f_copies[slot] = copy

        def send_g(src, slot, peer):
            copy = remote(
                block(g_all, src), block(g_all, slot), g_send.at[slot], g_recv.at[slot], peer
            )
            copy.start()
            g_copies[slot] = copy

        def forward(send, copies):
            for dx in (1, -1):
                copies[spot(dx, 0)].wait_recv()
                for d in (1, -1):
                    send(spot(dx, 0), spot(dx, -d), narrow_peer(d))

        own_sends = [(spot(-d, 0), wide_peer(d)) for d in (1, -1)]
        own_sends += [(spot(0, -d), narrow_peer(d)) for d in (1, -1)]
        for slot, peer in own_sends:
            send_geo(0, slot, peer)
        feat_in.wait()
        for slot, peer in own_sends:
            send_f(0, slot, peer)
        cot_in.wait()
        for slot, peer in own_sends:
            send_g(0, slot, peer)

        own_x[...] = jnp.broadcast_to(off[0:1], (particles, particles)).T
        own_y[...] = jnp.broadcast_to(off[1:2], (particles, particles)).T
        own_live[...] = jnp.broadcast_to(live, (particles, particles)).T

        def pair_rows(q):
            dx, dy = AROUND[q]
            there = geo[q]
            weight = there[2:3] * KERNEL_SCALE
            if q == 0:
                weight = weight * 2.0
            else:
                first = FLAGS + SLOT_SHIFTS.index((-dy, dx))
                second = FLAGS + SLOT_SHIFTS.index((dy, -dx))
                weight = weight * (
                    geo[spot(0, dy), first : first + 1] + geo[spot(dx, 0), second : second + 1]
                )
            rows_of[q, 0:1, :] = there[0:1] + float(dx)
            rows_of[q, 1:2, :] = there[1:2] + float(dy)
            rows_of[q, 2:3, :] = weight

        def pair_kernels(start, stop):
            for q in range(start, stop):
                pair_rows(q)
            chunks = particles // CHUNK

            @pl.loop(start * chunks, stop * chunks)
            def _(step):
                q = step // chunks
                r = pl.multiple_of(step % chunks * CHUNK, CHUNK)
                lanes = pl.ds(pl.multiple_of(q * particles, particles), particles)
                u = rows_of[q, 0:1, :] - own_x[pl.ds(r, CHUNK), :]
                v = rows_of[q, 1:2, :] - own_y[pl.ds(r, CHUNK), :]
                square = u * u + v * v
                triple = 3.0 * (square * lax.rsqrt(jnp.maximum(square, TINY)))
                window = jnp.maximum(1.0 - square, 0.0)
                window = window * window * rows_of[q, 2:3, :]
                wu = window * u
                wv = window * v
                for level in range(levels // 2):
                    bump = jnp.maximum(1.0 - jnp.abs(triple - float(level)), 0.0)
                    for part, value in ((0, wu), (1, wv)):
                        base = (2 * level + part) * particles
                        s_all[pl.ds(base + r, CHUNK), lanes] = (bump * value).astype(BF16)

        pair_kernels(0, 1)
        forward(send_geo, geo_copies)
        for dy in (1, -1):
            geo_copies[spot(0, dy)].wait_recv()
        pair_kernels(1, NEAR)
        forward(send_f, f_copies)
        for q in range(NEAR, len(AROUND)):
            geo_copies[q].wait_recv()
        pair_kernels(NEAR, len(AROUND))
        forward(send_g, g_copies)
        for dy in (1, -1):
            f_copies[spot(0, dy)].wait_recv()

        def with_ones(blocks):
            return jnp.concatenate([blocks, jnp.ones(blocks.shape, BF16)], axis=1)

        @pl.loop(0, levels // 2)
        def _(step):
            span = pl.ds(pl.multiple_of(step * 2 * particles, 2 * particles), 2 * particles)
            f_acc[span, :] = jnp.dot(
                s_all[span, 0:near], with_ones(f_all[0:near, :]), preferred_element_type=F32
            )

        for q in range(NEAR, len(AROUND)):
            f_copies[q].wait_recv()

        def finish_z(level, count):
            span = pl.ds(pl.multiple_of(level * particles, particles), count * particles)
            acc = f_acc[span, :] + jnp.dot(
                s_all[span, near:], with_ones(f_all[near:, :]), preferred_element_type=F32
            )
            f_acc[span, channels:] = acc[:, channels:]
            feat = f_all[0:particles, :].astype(F32)
            parts = []
            for j in range(count):
                mine = acc[j * particles : (j + 1) * particles]
                z = ((mine[:, channels:] * feat + mine[:, 0:channels]) * own_live[...]).astype(BF16)
                z_all[level + j] = z
                parts.append(
                    lax.dot_general(
                        z, g_all[0:particles, :], (((0,), (0,)), ((), ())),
                        preferred_element_type=F32,
                    ).astype(BF16)
                )
            return jnp.concatenate(parts, axis=0)

        def part_copy(d):
            peer = narrow_peer(d)
            return remote(
                w_part.at[peer[1]], n_in.at[d - 1], ns_send.at[d - 1], ns_recv.at[d - 1], peer
            )

        if levels % nn == 0:
            each = levels // nn

            turn = 1 - 2 * lax.rem(mn, 2)

            @pl.loop(0, nn)
            def _(step):
                d = lax.rem(nn // 2 + nn + turn * step, nn)
                piece = narrow_peer(d)[1]
                w_part[piece] = finish_z(piece * each, each)

                @pl.when(d > 0)
                def _():
                    part_copy(d).start()
        else:
            split = nn // levels
            assert split * levels == nn

            @pl.loop(0, levels)
            def _(level):
                part = finish_z(level, 1)
                for j in range(split):
                    w_part[level * split + j] = part[j * rows_n : (j + 1) * rows_n]

            @pl.loop(1, nn)
            def _(d):
                part_copy(d).start()

        kern_in.wait()
        for dy in (1, -1):
            g_copies[spot(0, dy)].wait_recv()
        for q in range(NEAR, len(AROUND)):
            g_copies[q].wait_recv()
        force_out[...] = jnp.zeros_like(force_out)
        grad_out[...] = jnp.zeros_like(grad_out)

        def outputs_of(k):
            span = pl.ds(pl.multiple_of(k * particles, particles), particles)
            force_out[...] += jnp.dot(z_all[k], k_all[k], preferred_element_type=F32)
            acc = jnp.dot(s_all[span, :], g_all[...], preferred_element_type=F32)
            own = f_acc[span, channels:] * g_all[0:particles, :].astype(F32)
            y = ((own - acc) * own_live[...]).astype(BF16)
            grad_out[...] += lax.dot_general(
                y, k_all[k], (((1,), (1,)), ((), ())), preferred_element_type=F32
            )

        cuts = [0, levels // 4, levels // 2, levels * 5 // 8, levels]

        def outputs_stage(stage):
            pl.loop(cuts[stage], cuts[stage + 1])(outputs_of)

        def send_outputs():
            corrected_out = f_all.at[pl.ds(0, particles)]
            for copies in (f_copies, g_copies, geo_copies):
                for copy in copies.values():
                    copy.wait_send()
            corrected_out[...] = force_out[...].astype(BF16)
            force_copy = pltpu.make_async_copy(corrected_out, corrected_ref.at[0, 0], out_sem.at[0])
            grad_copy = pltpu.make_async_copy(grad_out, grad_ref.at[0, 0], out_sem.at[1])
            force_copy.start()
            grad_copy.start()
            return force_copy, grad_copy

        outputs_stage(0)

        total = w_part[mn].astype(F32)
        for d in range(1, nn):
            part_copy(d).wait_recv()
            total += n_in[d - 1].astype(F32)

        def row_copy(d, step):
            at = lax.rem(mw - step + nw, nw) if scattered else 0
            return remote(
                w_out.at[at], n_out.at[mn, at],
                na_send.at[d - 1, step], na_recv.at[d - 1, step], narrow_peer(d),
            )

        def send_row(step):
            for d in far_first:
                row_copy(d, step).start()

        if scattered:

            def scatter_copy(d):
                peer = wide_peer(d)
                return remote(
                    w_sum.at[peer[0]], w_in.at[d - 1], ws_send.at[d - 1], ws_recv.at[d - 1], peer
                )

            def column_copy(d):
                return remote(
                    w_out.at[mw], w_out.at[mw],
                    wa_send.at[d - 1], wa_recv.at[d - 1], wide_peer(d),
                )

            w_sum[...] = total.astype(BF16).reshape(nw, rows_w, channels)
            for d in range(1, nw):
                scatter_copy(d).start()
            outputs_stage(1)
            piece = w_sum[mw].astype(F32)
            for d in range(1, nw):
                scatter_copy(d).wait_recv()
                piece += w_in[d - 1].astype(F32)
            w_out[mw] = (piece * norm).astype(BF16)
            for d in range(1, nw):
                column_copy(d).start()
            send_row(0)
            outputs_stage(2)

            @pl.loop(1, nw)
            def _(turn):
                half = (turn + 1) // 2
                step = half + (turn + 1) % 2 * (nw - 2 * half)
                column_copy(step).wait_recv()
                send_row(step)

            @pl.loop(1, nw)
            def _(d):
                scatter_copy(d).wait_send()
                column_copy(d).wait_send()
        else:

            def scatter_copy(d):
                return remote(
                    w_in.at[mw], w_in.at[mw], ws_send.at[d - 1], ws_recv.at[d - 1], wide_peer(d)
                )

            w_in[mw] = total.astype(BF16)

            @pl.loop(1, nw)
            def _(d):
                scatter_copy(d).start()

            @pl.loop(1, nw)
            def _(d):
                scatter_copy(d).wait()

            outputs_stage(1)
            outputs_stage(2)
            w_out[0] = (jnp.sum(w_in[...].astype(F32), axis=0) * norm).astype(BF16)
            send_row(0)
        own_copy = pltpu.make_async_copy(w_out, n_out.at[mn], out_sem.at[2])
        own_copy.start()
        outputs_stage(3)
        force_copy, grad_copy = send_outputs()

        @pl.loop(1, nn)
        def _(d):
            part_copy(d).wait_send()

        @pl.loop(0, gathered[1])
        def _(step):
            for d in range(1, nn):
                row_copy(d, step).wait()

        force_copy.wait()
        grad_copy.wait()
        own_copy.wait()

    spots = len(AROUND)
    wide_in = (nw - 1, rows_w, channels) if scattered else (nw, rows_n, channels)
    wide_sum = (nw, rows_w, channels) if scattered else (1, 16, channels)
    dma = pltpu.SemaphoreType.DMA
    square = pltpu.VMEM((particles, particles), F32)
    block_sum = pltpu.VMEM((particles, channels), F32)
    scratch = [
        pltpu.VMEM((spots * particles, channels), BF16),
        pltpu.VMEM((spots * particles, channels), BF16),
        pltpu.VMEM((levels, channels, channels), BF16),
        pltpu.VMEM((spots, FLAGS + len(SLOT_SHIFTS), particles), F32),
        pltpu.VMEM((spots, FLAGS, particles), F32),
        pltpu.VMEM((levels * particles, spots * particles), BF16),
        pltpu.VMEM((levels * particles, 2 * channels), F32),
        square, square, square,
        pltpu.VMEM((levels, particles, channels), BF16),
        block_sum, block_sum,
        pltpu.VMEM((nn, rows_n, channels), BF16),
        pltpu.VMEM((nn - 1, rows_n, channels), BF16),
        pltpu.VMEM(wide_sum, BF16),
        pltpu.VMEM(wide_in, BF16),
        pltpu.VMEM(gathered[1:], BF16),
        dma((3,)), dma((3,)),
        dma((spots,)), dma((spots,)), dma((spots,)), dma((spots,)), dma((spots,)), dma((spots,)),
        dma((nn - 1,)), dma((nn - 1,)), dma((nw - 1,)), dma((nw - 1,)),
        dma((nw - 1,)), dma((nw - 1,)),
        dma((nn - 1, gathered[1])), dma((nn - 1, gathered[1])),
    ]
    return kernel, scratch, gathered


def deliver(
    corrected_in, grad_in, weights_in, corrected_ref, grad_ref, weights_ref,
    corrected, grad, narrow, wide, sems,
):
    loads = [
        pltpu.make_async_copy(weights_in, narrow, sems.at[0]),
        pltpu.make_async_copy(grad_in, grad, sems.at[1]),
        pltpu.make_async_copy(corrected_in, corrected, sems.at[2]),
    ]
    copies = [
        pltpu.make_async_copy(wide, weights_ref, sems.at[3]),
        pltpu.make_async_copy(grad, grad_ref, sems.at[4]),
        pltpu.make_async_copy(corrected, corrected_ref, sems.at[5]),
    ]
    for copy in loads:
        copy.start()
    loads[0].wait()
    wide[...] = narrow[...].astype(F32).reshape(wide.shape)
    copies[0].start()
    for load, copy in zip(loads[1:], copies[1:]):
        load.wait()
        copy.start()
    for copy in copies:
        copy.wait()


def body(features, offsets, counts, owned_pairs, kernels, cotangent):
    particles, channels = features.shape[2:]
    levels = kernels.shape[0]
    nw, nn = lax.axis_size("wide"), lax.axis_size("narrow")
    kernel, scratch, gathered = make_kernel(nw, nn, particles, channels, levels)
    vmem = pl.BlockSpec(memory_space=pltpu.VMEM)
    smem = pl.BlockSpec(memory_space=pltpu.SMEM)
    hbm = pl.BlockSpec(memory_space=pltpu.HBM)
    outs = (
        jax.ShapeDtypeStruct(features.shape, BF16),
        jax.ShapeDtypeStruct(features.shape, F32),
    )
    results = pl.pallas_call(
        kernel,
        out_shape=outs + (jax.ShapeDtypeStruct(gathered, BF16),),
        in_specs=[smem, smem, hbm, vmem, hbm, hbm],
        out_specs=(hbm, hbm, hbm),
        scratch_shapes=scratch,
        compiler_params=pltpu.CompilerParams(
            collective_id=0, has_side_effects=True, vmem_limit_bytes=VMEM_BYTES
        ),
        name="antisymmetric_convolution",
    )(counts, owned_pairs, features, offsets, kernels, cotangent)
    return pl.pallas_call(
        deliver,
        out_shape=outs + (jax.ShapeDtypeStruct(kernels.shape, F32),),
        in_specs=[hbm, hbm, hbm],
        out_specs=(hbm, hbm, hbm),
        scratch_shapes=[
            pltpu.VMEM(features.shape, BF16),
            pltpu.VMEM(features.shape, F32),
            pltpu.VMEM(gathered, BF16),
            pltpu.VMEM(kernels.shape, F32),
            pltpu.SemaphoreType.DMA((6,)),
        ],
        compiler_params=pltpu.CompilerParams(vmem_limit_bytes=VMEM_BYTES),
        name="deliver",
    )(*results)


def solution(mesh):
    placed = (
        P("wide", "narrow", None, None),
        P("wide", "narrow", None, None),
        P("wide", "narrow"),
        P("wide", "narrow", None),
        P(),
        P("wide", "narrow", None, None),
    )
    return jax.shard_map(
        body,
        mesh=mesh,
        in_specs=placed,
        out_specs=(P("wide", "narrow", None, None), P("wide", "narrow", None, None), P()),
        check_vma=False,
    )
```

```python
import math

import jax
import jax.numpy as jnp
from jax import lax
from jax.experimental import pallas as pl
from jax.experimental.pallas import tpu as pltpu
from jax.sharding import PartitionSpec as P

KERNEL_SCALE = 0.0625
SLOT_SHIFTS = ((0, 1), (0, -1), (-1, 0), (1, 0), (-1, 1), (1, -1), (1, 1), (-1, -1))
AROUND = ((0, 0), (-1, 0), (1, 0), (0, -1), (0, 1), (-1, -1), (-1, 1), (1, -1), (1, 1))
NEAR = 5
FLAGS = 8
CHUNK = 64
TINY = 1e-30
VMEM_BYTES = 56 * 1024 * 1024
F32 = jnp.float32
BF16 = jnp.bfloat16


def spot(dx, dy):
    return AROUND.index((dx, dy))


def make_kernel(nw, nn, particles, channels, levels):
    rows = levels * channels
    rows_n = rows // nn
    rows_w = rows_n // nw
    scattered = rows_w % 16 == 0 and rows_w > 0
    norm = 1.0 / math.sqrt(nw * nn * particles)
    near = NEAR * particles
    gathered = (nn, nw, rows_w, channels) if scattered else (nn, 1, rows_n, channels)
    far_first = sorted(range(1, nn), key=lambda d: -min(d, nn - d))

    def kernel(
        counts_ref, owned_ref, feat_ref, off_ref, kern_ref, cot_ref,
        corrected_ref, grad_ref, n_out,
        f_all, g_all, k_all, geo, rows_of, s_all, f_acc, own_x, own_y, own_live, z_all,
        force_out, grad_out, w_part, n_in, w_sum, w_in, w_out,
        in_sem, out_sem, f_send, f_recv, g_send, g_recv, p_send, p_recv,
        ns_send, ns_recv, ws_send, ws_recv, wa_send, wa_recv, na_send, na_recv,
    ):
        mw = lax.axis_index("wide")
        mn = lax.axis_index("narrow")

        def wide_peer(step):
            return (lax.rem(mw + step + nw, nw), mn)

        def narrow_peer(step):
            return (mw, lax.rem(mn + step + nn, nn))

        barrier = pltpu.get_barrier_semaphore()
        for d in range(1, nw):
            pl.semaphore_signal(
                barrier, inc=1, device_id=wide_peer(d), device_id_type=pl.DeviceIdType.MESH
            )
        for d in range(1, nn):
            pl.semaphore_signal(
                barrier, inc=1, device_id=narrow_peer(d), device_id_type=pl.DeviceIdType.MESH
            )

        def remote(src, dst, send, recv, peer):
            return pltpu.make_async_remote_copy(
                src_ref=src, dst_ref=dst, send_sem=send, recv_sem=recv,
                device_id=peer, device_id_type=pl.DeviceIdType.MESH,
            )

        def block(ref, q):
            return ref.at[pl.ds(q * particles, particles)]

        feat_in = pltpu.make_async_copy(feat_ref.at[0, 0], block(f_all, 0), in_sem.at[0])
        cot_in = pltpu.make_async_copy(cot_ref.at[0, 0], block(g_all, 0), in_sem.at[1])
        kern_in = pltpu.make_async_copy(kern_ref, k_all, in_sem.at[2])
        feat_in.start()
        cot_in.start()
        kern_in.start()

        off = off_ref[0, 0].astype(F32)
        lane = lax.broadcasted_iota(jnp.int32, (1, particles), 1)
        live = (lane < counts_ref[0, 0]).astype(F32)
        geo[0, 0:2, :] = off
        geo[0, 2:3, :] = live
        for s in range(len(SLOT_SHIFTS)):
            geo[0, FLAGS + s : FLAGS + s + 1, :] = jnp.full(
                (1, particles), owned_ref[0, 0, s].astype(F32)
            )

        pl.semaphore_wait(barrier, nw - 1 + nn - 1)

        geo_copies, f_copies, g_copies = {}, {}, {}

        def send_geo(src, slot, peer):
            copy = remote(geo.at[src], geo.at[slot], p_send.at[slot], p_recv.at[slot], peer)
            copy.start()
            geo_copies[slot] = copy

        def send_f(src, slot, peer):
            copy = remote(
                block(f_all, src), block(f_all, slot), f_send.at[slot], f_recv.at[slot], peer
            )
            copy.start()
            f_copies[slot] = copy

        def send_g(src, slot, peer):
            copy = remote(
                block(g_all, src), block(g_all, slot), g_send.at[slot], g_recv.at[slot], peer
            )
            copy.start()
            g_copies[slot] = copy

        def forward(send, copies):
            for dx in (1, -1):
                copies[spot(dx, 0)].wait_recv()
                for d in (1, -1):
                    send(spot(dx, 0), spot(dx, -d), narrow_peer(d))

        own_sends = [(spot(-d, 0), wide_peer(d)) for d in (1, -1)]
        own_sends += [(spot(0, -d), narrow_peer(d)) for d in (1, -1)]
        for slot, peer in own_sends:
            send_geo(0, slot, peer)
        feat_in.wait()
        for slot, peer in own_sends:
            send_f(0, slot, peer)
        cot_in.wait()
        for slot, peer in own_sends:
            send_g(0, slot, peer)

        own_x[...] = jnp.broadcast_to(off[0:1], (particles, particles)).T
        own_y[...] = jnp.broadcast_to(off[1:2], (particles, particles)).T
        own_live[...] = jnp.broadcast_to(live, (particles, particles)).T

        def pair_rows(q):
            dx, dy = AROUND[q]
            there = geo[q]
            weight = there[2:3] * KERNEL_SCALE
            if q == 0:
                weight = weight * 2.0
            else:
                first = FLAGS + SLOT_SHIFTS.index((-dy, dx))
                second = FLAGS + SLOT_SHIFTS.index((dy, -dx))
                weight = weight * (
                    geo[spot(0, dy), first : first + 1] + geo[spot(dx, 0), second : second + 1]
                )
            rows_of[q, 0:1, :] = there[0:1] + float(dx)
            rows_of[q, 1:2, :] = there[1:2] + float(dy)
            rows_of[q, 2:3, :] = weight

        def pair_kernels(start, stop):
            for q in range(start, stop):
                pair_rows(q)
            chunks = particles // CHUNK

            @pl.loop(start * chunks, stop * chunks)
            def _(step):
                q = step // chunks
                r = pl.multiple_of(step % chunks * CHUNK, CHUNK)
                lanes = pl.ds(pl.multiple_of(q * particles, particles), particles)
                u = rows_of[q, 0:1, :] - own_x[pl.ds(r, CHUNK), :]
                v = rows_of[q, 1:2, :] - own_y[pl.ds(r, CHUNK), :]
                square = u * u + v * v
                triple = 3.0 * (square * lax.rsqrt(jnp.maximum(square, TINY)))
                window = jnp.maximum(1.0 - square, 0.0)
                window = window * window * rows_of[q, 2:3, :]
                wu = window * u
                wv = window * v
                for level in range(levels // 2):
                    bump = jnp.maximum(1.0 - jnp.abs(triple - float(level)), 0.0)
                    for part, value in ((0, wu), (1, wv)):
                        base = (2 * level + part) * particles
                        s_all[pl.ds(base + r, CHUNK), lanes] = (bump * value).astype(BF16)

        pair_kernels(0, 1)
        forward(send_geo, geo_copies)
        for dy in (1, -1):
            geo_copies[spot(0, dy)].wait_recv()
        pair_kernels(1, NEAR)
        forward(send_f, f_copies)
        for q in range(NEAR, len(AROUND)):
            geo_copies[q].wait_recv()
        pair_kernels(NEAR, len(AROUND))
        forward(send_g, g_copies)
        for dy in (1, -1):
            f_copies[spot(0, dy)].wait_recv()

        def with_ones(blocks):
            return jnp.concatenate([blocks, jnp.ones(blocks.shape, BF16)], axis=1)

        @pl.loop(0, levels // 2)
        def _(step):
            span = pl.ds(pl.multiple_of(step * 2 * particles, 2 * particles), 2 * particles)
            f_acc[span, :] = jnp.dot(
                s_all[span, 0:near], with_ones(f_all[0:near, :]), preferred_element_type=F32
            )

        for q in range(NEAR, len(AROUND)):
            f_copies[q].wait_recv()

        def finish_z(level, count):
            span = pl.ds(pl.multiple_of(level * particles, particles), count * particles)
            acc = f_acc[span, :] + jnp.dot(
                s_all[span, near:], with_ones(f_all[near:, :]), preferred_element_type=F32
            )
            f_acc[span, channels:] = acc[:, channels:]
            feat = f_all[0:particles, :].astype(F32)
            parts = []
            for j in range(count):
                mine = acc[j * particles : (j + 1) * particles]
                z = ((mine[:, channels:] * feat + mine[:, 0:channels]) * own_live[...]).astype(BF16)
                z_all[level + j] = z
                parts.append(
                    lax.dot_general(
                        z, g_all[0:particles, :], (((0,), (0,)), ((), ())),
                        preferred_element_type=F32,
                    ).astype(BF16)
                )
            return jnp.concatenate(parts, axis=0)

        def part_copy(d):
            peer = narrow_peer(d)
            return remote(
                w_part.at[peer[1]], n_in.at[d - 1], ns_send.at[d - 1], ns_recv.at[d - 1], peer
            )

        if levels % nn == 0:
            each = levels // nn

            @pl.loop(1, nn + 1)
            def _(d):
                piece = narrow_peer(d)[1]
                w_part[piece] = finish_z(piece * each, each)

                @pl.when(d < nn)
                def _():
                    part_copy(d).start()
        else:
            split = nn // levels
            assert split * levels == nn

            @pl.loop(0, levels)
            def _(level):
                part = finish_z(level, 1)
                for j in range(split):
                    w_part[level * split + j] = part[j * rows_n : (j + 1) * rows_n]

            @pl.loop(1, nn)
            def _(d):
                part_copy(d).start()

        kern_in.wait()
        for dy in (1, -1):
            g_copies[spot(0, dy)].wait_recv()
        for q in range(NEAR, len(AROUND)):
            g_copies[q].wait_recv()
        force_out[...] = jnp.zeros_like(force_out)
        grad_out[...] = jnp.zeros_like(grad_out)

        def outputs_of(k):
            span = pl.ds(pl.multiple_of(k * particles, particles), particles)
            force_out[...] += jnp.dot(z_all[k], k_all[k], preferred_element_type=F32)
            acc = jnp.dot(s_all[span, :], g_all[...], preferred_element_type=F32)
            own = f_acc[span, channels:] * g_all[0:particles, :].astype(F32)
            y = ((own - acc) * own_live[...]).astype(BF16)
            grad_out[...] += lax.dot_general(
                y, k_all[k], (((1,), (1,)), ((), ())), preferred_element_type=F32
            )

        cuts = [0, levels * 3 // 8, levels * 6 // 8, levels]

        def outputs_stage(stage):
            pl.loop(cuts[stage], cuts[stage + 1])(outputs_of)

        def send_outputs():
            corrected_out = f_all.at[pl.ds(0, particles)]
            for copies in (f_copies, g_copies, geo_copies):
                for copy in copies.values():
                    copy.wait_send()
            corrected_out[...] = force_out[...].astype(BF16)
            force_copy = pltpu.make_async_copy(corrected_out, corrected_ref.at[0, 0], out_sem.at[0])
            grad_copy = pltpu.make_async_copy(grad_out, grad_ref.at[0, 0], out_sem.at[1])
            force_copy.start()
            grad_copy.start()
            return force_copy, grad_copy

        outputs_stage(0)

        total = w_part[mn].astype(F32)
        for d in range(1, nn):
            part_copy(d).wait_recv()
            total += n_in[d - 1].astype(F32)

        def row_copy(d, step):
            return remote(
                w_out, n_out.at[mn], na_send.at[d - 1, step], na_recv.at[d - 1, step], narrow_peer(d)
            )

        def send_row(step):
            for d in far_first:
                row_copy(d, step).start()

        if scattered:

            def scatter_copy(d):
                peer = wide_peer(d)
                return remote(
                    w_sum.at[peer[0]], w_in.at[d - 1], ws_send.at[d - 1], ws_recv.at[d - 1], peer
                )

            def column_copy(d):
                return remote(
                    w_out.at[mw], w_out.at[mw],
                    wa_send.at[d - 1], wa_recv.at[d - 1], wide_peer(d),
                )

            w_sum[...] = total.astype(BF16).reshape(nw, rows_w, channels)
            for d in range(1, nw):
                scatter_copy(d).start()
            outputs_stage(1)
            piece = w_sum[mw].astype(F32)
            for d in range(1, nw):
                scatter_copy(d).wait_recv()
                piece += w_in[d - 1].astype(F32)
            w_out[mw] = (piece * norm).astype(BF16)
            for d in range(1, nw):
                column_copy(d).start()
            outputs_stage(2)

            @pl.loop(1, nw)
            def _(step):
                column_copy(step).wait_recv()

            send_row(0)
            force_copy, grad_copy = send_outputs()

            @pl.loop(1, nw)
            def _(d):
                scatter_copy(d).wait_send()
                column_copy(d).wait_send()
        else:

            def scatter_copy(d):
                return remote(
                    w_in.at[mw], w_in.at[mw], ws_send.at[d - 1], ws_recv.at[d - 1], wide_peer(d)
                )

            w_in[mw] = total.astype(BF16)

            @pl.loop(1, nw)
            def _(d):
                scatter_copy(d).start()

            @pl.loop(1, nw)
            def _(d):
                scatter_copy(d).wait()

            outputs_stage(1)
            outputs_stage(2)
            force_copy, grad_copy = send_outputs()
            w_out[0] = (jnp.sum(w_in[...].astype(F32), axis=0) * norm).astype(BF16)
            send_row(0)
        own_copy = pltpu.make_async_copy(w_out, n_out.at[mn], out_sem.at[2])
        own_copy.start()

        @pl.loop(1, nn)
        def _(d):
            part_copy(d).wait_send()

        for d in range(1, nn):
            row_copy(d, 0).wait()

        force_copy.wait()
        grad_copy.wait()
        own_copy.wait()

    spots = len(AROUND)
    wide_in = (nw - 1, rows_w, channels) if scattered else (nw, rows_n, channels)
    wide_sum = (nw, rows_w, channels) if scattered else (1, 16, channels)
    dma = pltpu.SemaphoreType.DMA
    square = pltpu.VMEM((particles, particles), F32)
    block_sum = pltpu.VMEM((particles, channels), F32)
    scratch = [
        pltpu.VMEM((spots * particles, channels), BF16),
        pltpu.VMEM((spots * particles, channels), BF16),
        pltpu.VMEM((levels, channels, channels), BF16),
        pltpu.VMEM((spots, FLAGS + len(SLOT_SHIFTS), particles), F32),
        pltpu.VMEM((spots, FLAGS, particles), F32),
        pltpu.VMEM((levels * particles, spots * particles), BF16),
        pltpu.VMEM((levels * particles, 2 * channels), F32),
        square, square, square,
        pltpu.VMEM((levels, particles, channels), BF16),
        block_sum, block_sum,
        pltpu.VMEM((nn, rows_n, channels), BF16),
        pltpu.VMEM((nn - 1, rows_n, channels), BF16),
        pltpu.VMEM(wide_sum, BF16),
        pltpu.VMEM(wide_in, BF16),
        pltpu.VMEM(gathered[1:], BF16),
        dma((3,)), dma((3,)),
        dma((spots,)), dma((spots,)), dma((spots,)), dma((spots,)), dma((spots,)), dma((spots,)),
        dma((nn - 1,)), dma((nn - 1,)), dma((nw - 1,)), dma((nw - 1,)),
        dma((nw - 1,)), dma((nw - 1,)),
        dma((nn - 1, 1)), dma((nn - 1, 1)),
    ]
    return kernel, scratch, gathered


def deliver(
    corrected_in, grad_in, weights_in, corrected_ref, grad_ref, weights_ref,
    corrected, grad, narrow, wide, sems,
):
    loads = [
        pltpu.make_async_copy(weights_in, narrow, sems.at[0]),
        pltpu.make_async_copy(grad_in, grad, sems.at[1]),
        pltpu.make_async_copy(corrected_in, corrected, sems.at[2]),
    ]
    copies = [
        pltpu.make_async_copy(wide, weights_ref, sems.at[3]),
        pltpu.make_async_copy(grad, grad_ref, sems.at[4]),
        pltpu.make_async_copy(corrected, corrected_ref, sems.at[5]),
    ]
    for copy in loads:
        copy.start()
    loads[0].wait()
    wide[...] = narrow[...].astype(F32).reshape(wide.shape)
    copies[0].start()
    for load, copy in zip(loads[1:], copies[1:]):
        load.wait()
        copy.start()
    for copy in copies:
        copy.wait()


def body(features, offsets, counts, owned_pairs, kernels, cotangent):
    particles, channels = features.shape[2:]
    levels = kernels.shape[0]
    nw, nn = lax.axis_size("wide"), lax.axis_size("narrow")
    kernel, scratch, gathered = make_kernel(nw, nn, particles, channels, levels)
    vmem = pl.BlockSpec(memory_space=pltpu.VMEM)
    smem = pl.BlockSpec(memory_space=pltpu.SMEM)
    hbm = pl.BlockSpec(memory_space=pltpu.HBM)
    outs = (
        jax.ShapeDtypeStruct(features.shape, BF16),
        jax.ShapeDtypeStruct(features.shape, F32),
    )
    results = pl.pallas_call(
        kernel,
        out_shape=outs + (jax.ShapeDtypeStruct(gathered, BF16),),
        in_specs=[smem, smem, hbm, vmem, hbm, hbm],
        out_specs=(hbm, hbm, hbm),
        scratch_shapes=scratch,
        compiler_params=pltpu.CompilerParams(
            collective_id=0, has_side_effects=True, vmem_limit_bytes=VMEM_BYTES
        ),
        name="antisymmetric_convolution",
    )(counts, owned_pairs, features, offsets, kernels, cotangent)
    return pl.pallas_call(
        deliver,
        out_shape=outs + (jax.ShapeDtypeStruct(kernels.shape, F32),),
        in_specs=[hbm, hbm, hbm],
        out_specs=(hbm, hbm, hbm),
        scratch_shapes=[
            pltpu.VMEM(features.shape, BF16),
            pltpu.VMEM(features.shape, F32),
            pltpu.VMEM(gathered, BF16),
            pltpu.VMEM(kernels.shape, F32),
            pltpu.SemaphoreType.DMA((6,)),
        ],
        compiler_params=pltpu.CompilerParams(vmem_limit_bytes=VMEM_BYTES),
        name="deliver",
    )(*results)


def solution(mesh):
    placed = (
        P("wide", "narrow", None, None),
        P("wide", "narrow", None, None),
        P("wide", "narrow"),
        P("wide", "narrow", None),
        P(),
        P("wide", "narrow", None, None),
    )
    return jax.shard_map(
        body,
        mesh=mesh,
        in_specs=placed,
        out_specs=(P("wide", "narrow", None, None), P("wide", "narrow", None, None), P()),
        check_vma=False,
    )
```

```python
import math

import jax
import jax.numpy as jnp
from jax import lax
from jax.experimental import pallas as pl
from jax.experimental.pallas import tpu as pltpu
from jax.sharding import PartitionSpec as P

KERNEL_SCALE = 0.0625
SLOT_SHIFTS = ((0, 1), (0, -1), (-1, 0), (1, 0), (-1, 1), (1, -1), (1, 1), (-1, -1))
AROUND = ((0, 0), (-1, 0), (1, 0), (0, -1), (0, 1), (-1, -1), (-1, 1), (1, -1), (1, 1))
NEAR = 5
FLAGS = 8
CHUNK = 64
TINY = 1e-30
VMEM_BYTES = 56 * 1024 * 1024
F32 = jnp.float32
BF16 = jnp.bfloat16


def spot(dx, dy):
    return AROUND.index((dx, dy))


def make_kernel(nw, nn, particles, channels, levels):
    rows = levels * channels
    rows_n = rows // nn
    rows_w = rows_n // nw
    scattered = rows_w % 16 == 0 and rows_w > 0
    norm = 1.0 / math.sqrt(nw * nn * particles)
    near = NEAR * particles
    gathered = (nn, nw, rows_w, channels) if scattered else (nn, 1, rows_n, channels)
    far_first = sorted(range(1, nn), key=lambda d: -min(d, nn - d))

    def kernel(
        counts_ref, owned_ref, feat_ref, off_ref, kern_ref, cot_ref,
        corrected_ref, grad_ref, n_out,
        f_all, g_all, k_all, geo, rows_of, s_all, f_acc, own_x, own_y, own_live, z_all,
        force_out, grad_out, w_part, n_in, w_sum, w_in, w_out,
        in_sem, out_sem, f_send, f_recv, g_send, g_recv, p_send, p_recv,
        ns_send, ns_recv, ws_send, ws_recv, wa_send, wa_recv, na_send, na_recv,
    ):
        mw = lax.axis_index("wide")
        mn = lax.axis_index("narrow")

        def wide_peer(step):
            return (lax.rem(mw + step + nw, nw), mn)

        def narrow_peer(step):
            return (mw, lax.rem(mn + step + nn, nn))

        barrier = pltpu.get_barrier_semaphore()
        for d in range(1, nw):
            pl.semaphore_signal(
                barrier, inc=1, device_id=wide_peer(d), device_id_type=pl.DeviceIdType.MESH
            )
        for d in range(1, nn):
            pl.semaphore_signal(
                barrier, inc=1, device_id=narrow_peer(d), device_id_type=pl.DeviceIdType.MESH
            )

        def remote(src, dst, send, recv, peer):
            return pltpu.make_async_remote_copy(
                src_ref=src, dst_ref=dst, send_sem=send, recv_sem=recv,
                device_id=peer, device_id_type=pl.DeviceIdType.MESH,
            )

        def block(ref, q):
            return ref.at[pl.ds(q * particles, particles)]

        feat_in = pltpu.make_async_copy(feat_ref.at[0, 0], block(f_all, 0), in_sem.at[0])
        cot_in = pltpu.make_async_copy(cot_ref.at[0, 0], block(g_all, 0), in_sem.at[1])
        kern_in = pltpu.make_async_copy(kern_ref, k_all, in_sem.at[2])
        feat_in.start()
        cot_in.start()
        kern_in.start()

        off = off_ref[0, 0].astype(F32)
        lane = lax.broadcasted_iota(jnp.int32, (1, particles), 1)
        live = (lane < counts_ref[0, 0]).astype(F32)
        geo[0, 0:2, :] = off
        geo[0, 2:3, :] = live
        for s in range(len(SLOT_SHIFTS)):
            geo[0, FLAGS + s : FLAGS + s + 1, :] = jnp.full(
                (1, particles), owned_ref[0, 0, s].astype(F32)
            )

        pl.semaphore_wait(barrier, nw - 1 + nn - 1)

        geo_copies, f_copies, g_copies = {}, {}, {}

        def send_geo(src, slot, peer):
            copy = remote(geo.at[src], geo.at[slot], p_send.at[slot], p_recv.at[slot], peer)
            copy.start()
            geo_copies[slot] = copy

        def send_f(src, slot, peer):
            copy = remote(
                block(f_all, src), block(f_all, slot), f_send.at[slot], f_recv.at[slot], peer
            )
            copy.start()
            f_copies[slot] = copy

        def send_g(src, slot, peer):
            copy = remote(
                block(g_all, src), block(g_all, slot), g_send.at[slot], g_recv.at[slot], peer
            )
            copy.start()
            g_copies[slot] = copy

        def forward(send, copies):
            for dx in (1, -1):
                copies[spot(dx, 0)].wait_recv()
                for d in (1, -1):
                    send(spot(dx, 0), spot(dx, -d), narrow_peer(d))

        own_sends = [(spot(-d, 0), wide_peer(d)) for d in (1, -1)]
        own_sends += [(spot(0, -d), narrow_peer(d)) for d in (1, -1)]
        for slot, peer in own_sends:
            send_geo(0, slot, peer)
        feat_in.wait()
        for slot, peer in own_sends:
            send_f(0, slot, peer)
        cot_in.wait()
        for slot, peer in own_sends:
            send_g(0, slot, peer)

        own_x[...] = jnp.broadcast_to(off[0:1], (particles, particles)).T
        own_y[...] = jnp.broadcast_to(off[1:2], (particles, particles)).T
        own_live[...] = jnp.broadcast_to(live, (particles, particles)).T

        def pair_rows(q):
            dx, dy = AROUND[q]
            there = geo[q]
            weight = there[2:3] * KERNEL_SCALE
            if q == 0:
                weight = weight * 2.0
            else:
                first = FLAGS + SLOT_SHIFTS.index((-dy, dx))
                second = FLAGS + SLOT_SHIFTS.index((dy, -dx))
                weight = weight * (
                    geo[spot(0, dy), first : first + 1] + geo[spot(dx, 0), second : second + 1]
                )
            rows_of[q, 0:1, :] = there[0:1] + float(dx)
            rows_of[q, 1:2, :] = there[1:2] + float(dy)
            rows_of[q, 2:3, :] = weight

        def pair_kernels(start, stop):
            for q in range(start, stop):
                pair_rows(q)
            chunks = particles // CHUNK

            @pl.loop(start * chunks, stop * chunks)
            def _(step):
                q = step // chunks
                r = pl.multiple_of(step % chunks * CHUNK, CHUNK)
                lanes = pl.ds(pl.multiple_of(q * particles, particles), particles)
                u = rows_of[q, 0:1, :] - own_x[pl.ds(r, CHUNK), :]
                v = rows_of[q, 1:2, :] - own_y[pl.ds(r, CHUNK), :]
                square = u * u + v * v
                triple = 3.0 * (square * lax.rsqrt(jnp.maximum(square, TINY)))
                window = jnp.maximum(1.0 - square, 0.0)
                window = window * window * rows_of[q, 2:3, :]
                wu = window * u
                wv = window * v
                for level in range(levels // 2):
                    bump = jnp.maximum(1.0 - jnp.abs(triple - float(level)), 0.0)
                    for part, value in ((0, wu), (1, wv)):
                        base = (2 * level + part) * particles
                        s_all[pl.ds(base + r, CHUNK), lanes] = (bump * value).astype(BF16)

        pair_kernels(0, 1)
        forward(send_geo, geo_copies)
        for dy in (1, -1):
            geo_copies[spot(0, dy)].wait_recv()
        pair_kernels(1, NEAR)
        forward(send_f, f_copies)
        for q in range(NEAR, len(AROUND)):
            geo_copies[q].wait_recv()
        pair_kernels(NEAR, len(AROUND))
        forward(send_g, g_copies)
        for dy in (1, -1):
            f_copies[spot(0, dy)].wait_recv()

        def with_ones(blocks):
            return jnp.concatenate([blocks, jnp.ones(blocks.shape, BF16)], axis=1)

        @pl.loop(0, levels // 2)
        def _(step):
            span = pl.ds(pl.multiple_of(step * 2 * particles, 2 * particles), 2 * particles)
            f_acc[span, :] = jnp.dot(
                s_all[span, 0:near], with_ones(f_all[0:near, :]), preferred_element_type=F32
            )

        for q in range(NEAR, len(AROUND)):
            f_copies[q].wait_recv()

        def finish_z(level, count):
            span = pl.ds(pl.multiple_of(level * particles, particles), count * particles)
            acc = f_acc[span, :] + jnp.dot(
                s_all[span, near:], with_ones(f_all[near:, :]), preferred_element_type=F32
            )
            f_acc[span, channels:] = acc[:, channels:]
            feat = f_all[0:particles, :].astype(F32)
            parts = []
            for j in range(count):
                mine = acc[j * particles : (j + 1) * particles]
                z = ((mine[:, channels:] * feat + mine[:, 0:channels]) * own_live[...]).astype(BF16)
                z_all[level + j] = z
                parts.append(
                    lax.dot_general(
                        z, g_all[0:particles, :], (((0,), (0,)), ((), ())),
                        preferred_element_type=F32,
                    ).astype(BF16)
                )
            return jnp.concatenate(parts, axis=0)

        def part_copy(d):
            peer = narrow_peer(d)
            return remote(
                w_part.at[peer[1]], n_in.at[d - 1], ns_send.at[d - 1], ns_recv.at[d - 1], peer
            )

        if levels % nn == 0:
            each = levels // nn

            @pl.loop(1, nn + 1)
            def _(d):
                piece = narrow_peer(d)[1]
                w_part[piece] = finish_z(piece * each, each)

                @pl.when(d < nn)
                def _():
                    part_copy(d).start()
        else:
            split = nn // levels
            assert split * levels == nn

            @pl.loop(0, levels)
            def _(level):
                part = finish_z(level, 1)
                for j in range(split):
                    w_part[level * split + j] = part[j * rows_n : (j + 1) * rows_n]

            @pl.loop(1, nn)
            def _(d):
                part_copy(d).start()

        kern_in.wait()
        for dy in (1, -1):
            g_copies[spot(0, dy)].wait_recv()
        for q in range(NEAR, len(AROUND)):
            g_copies[q].wait_recv()
        force_out[...] = jnp.zeros_like(force_out)
        grad_out[...] = jnp.zeros_like(grad_out)

        def outputs_of(k):
            span = pl.ds(pl.multiple_of(k * particles, particles), particles)
            force_out[...] += jnp.dot(z_all[k], k_all[k], preferred_element_type=F32)
            acc = jnp.dot(s_all[span, :], g_all[...], preferred_element_type=F32)
            own = f_acc[span, channels:] * g_all[0:particles, :].astype(F32)
            y = ((own - acc) * own_live[...]).astype(BF16)
            grad_out[...] += lax.dot_general(
                y, k_all[k], (((1,), (1,)), ((), ())), preferred_element_type=F32
            )

        cuts = [0, levels // 4, levels // 2, levels]

        def outputs_stage(stage):
            pl.loop(cuts[stage], cuts[stage + 1])(outputs_of)

        def send_outputs():
            corrected_out = f_all.at[pl.ds(0, particles)]
            for copies in (f_copies, g_copies, geo_copies):
                for copy in copies.values():
                    copy.wait_send()
            corrected_out[...] = force_out[...].astype(BF16)
            force_copy = pltpu.make_async_copy(corrected_out, corrected_ref.at[0, 0], out_sem.at[0])
            grad_copy = pltpu.make_async_copy(grad_out, grad_ref.at[0, 0], out_sem.at[1])
            force_copy.start()
            grad_copy.start()
            return force_copy, grad_copy

        outputs_stage(0)

        total = w_part[mn].astype(F32)
        for d in range(1, nn):
            part_copy(d).wait_recv()
            total += n_in[d - 1].astype(F32)

        def row_copy(d, step):
            return remote(
                w_out, n_out.at[mn], na_send.at[d - 1, step], na_recv.at[d - 1, step], narrow_peer(d)
            )

        def send_row(step):
            for d in far_first:
                row_copy(d, step).start()

        if scattered:

            def scatter_copy(d):
                peer = wide_peer(d)
                return remote(
                    w_sum.at[peer[0]], w_in.at[d - 1], ws_send.at[d - 1], ws_recv.at[d - 1], peer
                )

            def column_copy(d):
                return remote(
                    w_out.at[mw], w_out.at[mw],
                    wa_send.at[d - 1], wa_recv.at[d - 1], wide_peer(d),
                )

            w_sum[...] = total.astype(BF16).reshape(nw, rows_w, channels)
            for d in range(1, nw):
                scatter_copy(d).start()
            outputs_stage(1)
            piece = w_sum[mw].astype(F32)
            for d in range(1, nw):
                scatter_copy(d).wait_recv()
                piece += w_in[d - 1].astype(F32)
            w_out[mw] = (piece * norm).astype(BF16)
            for d in range(1, nw):
                column_copy(d).start()

            @pl.loop(1, nw)
            def _(step):
                column_copy(step).wait_recv()

            send_row(0)
            outputs_stage(2)
            force_copy, grad_copy = send_outputs()

            @pl.loop(1, nw)
            def _(d):
                scatter_copy(d).wait_send()
                column_copy(d).wait_send()
        else:

            def scatter_copy(d):
                return remote(
                    w_in.at[mw], w_in.at[mw], ws_send.at[d - 1], ws_recv.at[d - 1], wide_peer(d)
                )

            w_in[mw] = total.astype(BF16)

            @pl.loop(1, nw)
            def _(d):
                scatter_copy(d).start()

            @pl.loop(1, nw)
            def _(d):
                scatter_copy(d).wait()

            outputs_stage(1)
            outputs_stage(2)
            force_copy, grad_copy = send_outputs()
            w_out[0] = (jnp.sum(w_in[...].astype(F32), axis=0) * norm).astype(BF16)
            send_row(0)
        own_copy = pltpu.make_async_copy(w_out, n_out.at[mn], out_sem.at[2])
        own_copy.start()

        @pl.loop(1, nn)
        def _(d):
            part_copy(d).wait_send()

        for d in range(1, nn):
            row_copy(d, 0).wait()

        force_copy.wait()
        grad_copy.wait()
        own_copy.wait()

    spots = len(AROUND)
    wide_in = (nw - 1, rows_w, channels) if scattered else (nw, rows_n, channels)
    wide_sum = (nw, rows_w, channels) if scattered else (1, 16, channels)
    dma = pltpu.SemaphoreType.DMA
    square = pltpu.VMEM((particles, particles), F32)
    block_sum = pltpu.VMEM((particles, channels), F32)
    scratch = [
        pltpu.VMEM((spots * particles, channels), BF16),
        pltpu.VMEM((spots * particles, channels), BF16),
        pltpu.VMEM((levels, channels, channels), BF16),
        pltpu.VMEM((spots, FLAGS + len(SLOT_SHIFTS), particles), F32),
        pltpu.VMEM((spots, FLAGS, particles), F32),
        pltpu.VMEM((levels * particles, spots * particles), BF16),
        pltpu.VMEM((levels * particles, 2 * channels), F32),
        square, square, square,
        pltpu.VMEM((levels, particles, channels), BF16),
        block_sum, block_sum,
        pltpu.VMEM((nn, rows_n, channels), BF16),
        pltpu.VMEM((nn - 1, rows_n, channels), BF16),
        pltpu.VMEM(wide_sum, BF16),
        pltpu.VMEM(wide_in, BF16),
        pltpu.VMEM(gathered[1:], BF16),
        dma((3,)), dma((3,)),
        dma((spots,)), dma((spots,)), dma((spots,)), dma((spots,)), dma((spots,)), dma((spots,)),
        dma((nn - 1,)), dma((nn - 1,)), dma((nw - 1,)), dma((nw - 1,)),
        dma((nw - 1,)), dma((nw - 1,)),
        dma((nn - 1, 1)), dma((nn - 1, 1)),
    ]
    return kernel, scratch, gathered


def deliver(
    corrected_in, grad_in, weights_in, corrected_ref, grad_ref, weights_ref,
    corrected, grad, narrow, wide, sems,
):
    loads = [
        pltpu.make_async_copy(weights_in, narrow, sems.at[0]),
        pltpu.make_async_copy(grad_in, grad, sems.at[1]),
        pltpu.make_async_copy(corrected_in, corrected, sems.at[2]),
    ]
    copies = [
        pltpu.make_async_copy(wide, weights_ref, sems.at[3]),
        pltpu.make_async_copy(grad, grad_ref, sems.at[4]),
        pltpu.make_async_copy(corrected, corrected_ref, sems.at[5]),
    ]
    for copy in loads:
        copy.start()
    loads[0].wait()
    wide[...] = narrow[...].astype(F32).reshape(wide.shape)
    copies[0].start()
    for load, copy in zip(loads[1:], copies[1:]):
        load.wait()
        copy.start()
    for copy in copies:
        copy.wait()


def body(features, offsets, counts, owned_pairs, kernels, cotangent):
    particles, channels = features.shape[2:]
    levels = kernels.shape[0]
    nw, nn = lax.axis_size("wide"), lax.axis_size("narrow")
    kernel, scratch, gathered = make_kernel(nw, nn, particles, channels, levels)
    vmem = pl.BlockSpec(memory_space=pltpu.VMEM)
    smem = pl.BlockSpec(memory_space=pltpu.SMEM)
    hbm = pl.BlockSpec(memory_space=pltpu.HBM)
    outs = (
        jax.ShapeDtypeStruct(features.shape, BF16),
        jax.ShapeDtypeStruct(features.shape, F32),
    )
    results = pl.pallas_call(
        kernel,
        out_shape=outs + (jax.ShapeDtypeStruct(gathered, BF16),),
        in_specs=[smem, smem, hbm, vmem, hbm, hbm],
        out_specs=(hbm, hbm, hbm),
        scratch_shapes=scratch,
        compiler_params=pltpu.CompilerParams(
            collective_id=0, has_side_effects=True, vmem_limit_bytes=VMEM_BYTES
        ),
        name="antisymmetric_convolution",
    )(counts, owned_pairs, features, offsets, kernels, cotangent)
    return pl.pallas_call(
        deliver,
        out_shape=outs + (jax.ShapeDtypeStruct(kernels.shape, F32),),
        in_specs=[hbm, hbm, hbm],
        out_specs=(hbm, hbm, hbm),
        scratch_shapes=[
            pltpu.VMEM(features.shape, BF16),
            pltpu.VMEM(features.shape, F32),
            pltpu.VMEM(gathered, BF16),
            pltpu.VMEM(kernels.shape, F32),
            pltpu.SemaphoreType.DMA((6,)),
        ],
        compiler_params=pltpu.CompilerParams(vmem_limit_bytes=VMEM_BYTES),
        name="deliver",
    )(*results)


def solution(mesh):
    placed = (
        P("wide", "narrow", None, None),
        P("wide", "narrow", None, None),
        P("wide", "narrow"),
        P("wide", "narrow", None),
        P(),
        P("wide", "narrow", None, None),
    )
    return jax.shard_map(
        body,
        mesh=mesh,
        in_specs=placed,
        out_specs=(P("wide", "narrow", None, None), P("wide", "narrow", None, None), P()),
        check_vma=False,
    )
```
